256 devices in a mesh: dp: 4 (over x), tm: 4 (over y_lo, core), height: 16 (over y_hi, z).
Axes of the slice: x: 4, y: 4 (y_hi: 2, y_lo: 2; y = y_hi * 2 + y_lo), z: 8, core: 2. Of those that a mesh axis runs over, the one named last changes fastest.
Arguments:
- latent: bfloat16 [4, 8, 64, 16, 512], P('dp', 'tm', 'height'), may hold values from -6 to 6
- out_grad: bfloat16 [4, 8, 128, 32, 256], P('dp', 'tm', 'height'), may hold values from -6 to 6
- w_first: bfloat16 [27, 512, 512], P(None, None, 'height'), may hold values from -0.0546875 to 0.0546875
- w_second: bfloat16 [27, 512, 256], replicated, may hold values from -0.0546875 to 0.0546875
Outputs:
- grad_input: bfloat16 [4, 8, 64, 16, 512], P('dp', 'tm', 'height')
- grad_w2: float32 [512, 27, 256], P(('tm', 'height'))
The draws below stay inside these ranges and needn't reach their ends.
All inputs are finite; a program needn't handle non-finite values.
Results may differ from the reference program's by a relative error of at most 0.017.
Values may be sent and summed in bfloat16 or wider, within the bound.
A program may use at most 128 MiB of HBM per device.

```python
import jax
import jax.numpy as jnp
from jax import lax

CH_IN = 512
CH_OUT = 256
TAPS = 27
COLS = 16
CLIPS = 4
FRAMES = 8
ROWS = 64


def block_scale(stream_key, dims, cuts, low, high):
    def one(axis_at, shards_of):
        heights = jax.random.uniform(jax.random.fold_in(jax.random.fold_in(stream_key, 6), axis_at), (shards_of,), jnp.float32, low / len(cuts), high / len(cuts))
        return jnp.repeat(jnp.exp(heights), dims[axis_at] // shards_of).reshape((-1,) + (1,) * (len(dims) - axis_at - 1))

    loudness = one(*cuts[0])
    for cut in cuts[1:]:
        loudness = loudness * one(*cut)
    return loudness


def bell_draw(stream_key, dims, scale, most, shards=(), held_as=jnp.bfloat16):
    entries = jax.random.normal(stream_key, dims, jnp.float32) * scale
    if len(shards) > 0:
        entries = block_scale(stream_key, dims, shards, -0.22, 0.18) * entries
    return jnp.clip(entries, min=-most, max=most).astype(held_as)


def setup_inputs(seed: int = 0) -> dict:
    arg_keys = jax.random.split(jax.random.key(seed), 5)
    latent = bell_draw(arg_keys[0], (CLIPS, FRAMES, ROWS, COLS, CH_IN), 1.0, 6.0, ((0, 4), (1, 4), (2, 16)))
    out_grad = bell_draw(arg_keys[1], (CLIPS, FRAMES, 2 * ROWS, 2 * COLS, CH_OUT), 1.0, 6.0, ((0, 4), (1, 4), (2, 16)))
    w_first = bell_draw(arg_keys[2], (TAPS, CH_IN, CH_IN), (TAPS * CH_IN) ** -0.5, 0.0546875, ((2, 16),))
    w_second = bell_draw(arg_keys[3], (TAPS, CH_IN, CH_OUT), (TAPS * CH_IN) ** -0.5, 0.0546875)
    return {"latent": latent, "out_grad": out_grad, "w_first": w_first, "w_second": w_second}


def convolve(padded, kernel, layout):
    result = lax.conv_general_dilated(padded[None], kernel, (1, 1, 1), "VALID", dimension_numbers=("NDHWC", layout, "NDHWC"), precision=lax.Precision.HIGHEST, preferred_element_type=jnp.float32)
    return result[0]


def silu_slope(values):
    sigmoid_v = jax.nn.sigmoid(values)
    return sigmoid_v * (1.0 + values * (1.0 - sigmoid_v))


def clip_grads(latent, out_grad, kernel_one, kernel_two):
    frames, row_count, col_count, in_width = latent.shape
    padded = jnp.pad(latent.astype(jnp.float32), ((2, 0), (1, 1), (1, 1), (0, 0)))
    pre_act = convolve(padded, kernel_one, "DHWIO")
    act_out = jax.nn.silu(pre_act).astype(jnp.bfloat16)
    upsampled = jnp.repeat(jnp.repeat(act_out, 2, axis=1), 2, axis=2).astype(jnp.float32)
    cot_float = out_grad.astype(jnp.float32)
    cot_padded = jnp.pad(cot_float, ((0, 2), (1, 1), (1, 1), (0, 0)))
    grad_up = convolve(cot_padded, lax.rev(kernel_two, (0, 1, 2)), "DHWOI")
    grad_act = grad_up.reshape(frames, row_count, 2, col_count, 2, in_width).sum(axis=(2, 4))
    grad_pre = (grad_act * silu_slope(pre_act)).astype(jnp.bfloat16)
    pre_padded = jnp.pad(grad_pre.astype(jnp.float32), ((0, 2), (1, 1), (1, 1), (0, 0)))
    grad_in = convolve(pre_padded, lax.rev(kernel_one, (0, 1, 2)), "DHWOI").astype(jnp.bfloat16)
    up_padded = jnp.pad(upsampled, ((2, 0), (1, 1), (1, 1), (0, 0)))
    tap_terms = []
    for depth_tap in range(3):
        for row_tap in range(3):
            for col_tap in range(3):
                window = up_padded[depth_tap:depth_tap + frames, row_tap:row_tap + 2 * row_count, col_tap:col_tap + 2 * col_count]
                tap_terms.append(jnp.einsum("thci,thco->io", window, cot_float, precision=lax.Precision.HIGHEST))
    return grad_in, jnp.stack(tap_terms, axis=1)


def reference(latent, out_grad, w_first, w_second):
    kernel_one = w_first.astype(jnp.float32).reshape(3, 3, 3, CH_IN, CH_IN)
    kernel_two = w_second.astype(jnp.float32).reshape(3, 3, 3, CH_IN, CH_OUT)

    def per_clip(inputs):
        return clip_grads(inputs[0], inputs[1], kernel_one, kernel_two)

    grad_input, weight_parts = lax.map(per_clip, (latent, out_grad))
    rescale = 1.0 / (float(CLIPS * FRAMES * 4 * ROWS * COLS) ** 0.5)
    grad_w2 = jnp.sum(weight_parts, axis=0) * rescale
    return grad_input, grad_w2
```

```python
import functools
import math

import jax
import jax.numpy as jnp
import numpy as np
from jax import lax
from jax.experimental import pallas as pl
from jax.experimental.pallas import tpu as pltpu
from jax.sharding import PartitionSpec as P

MESH = pl.DeviceIdType.MESH
BF = jnp.bfloat16
F32 = jnp.float32
NZ = 8
NT = (((1,), (1,)), ((), ()))
NN = (((1,), (0,)), ((), ()))


def cell_sums():
    main = np.zeros((3, 3, 4, 16, 8, 32), np.float32)
    edge = np.zeros((2, 3, 16, 8, 32), np.float32)
    for b in range(3):
        for e in range(3):
            for c in range(16):
                cols = [2 * c + q + 1 - e for q in range(2) if 0 <= 2 * c + q + 1 - e < 32]
                for h in range(4):
                    for p in range(2):
                        row = 2 * h + p + 1 - b
                        if 0 <= row < 8:
                            main[b, e, h, c, row, cols] = 1.0
                if b == 0:
                    edge[0, e, c, 0, cols] = 1.0
                if b == 2:
                    edge[1, e, c, 7, cols] = 1.0
    return np.concatenate([main.reshape(576, 256), edge.reshape(96, 256)], axis=0)


def dot(a, b, dims):
    return lax.dot_general(a, b, dims, preferred_element_type=F32)


def body(
    scale,
    lat_in, og_in, wt_in, w2_in, sums_in, eye_in,
    gi_out, gw_out,
    xg, og, w, w2, g, gh, acc, q, qh, pre, ga, e1s, e1r, e2s, e2r,
    act, gp3, act3, act3t, hal3t, gi, pb, rp, ps, rr, gws, ra, sb, rb, fc, rc,
    ag_s, ag_r, wr_s, wr_r, wl_s, wl_r, w2_s, loc_s, e_s, e_r, pr_s, pr_r, rs_s, rs_r,
    a_s, a_r, b_s, b_r, c_s, c_r,
):
    x = lax.axis_index("dp")
    tm = lax.axis_index("tm")
    height = lax.axis_index("height")
    c = tm % 2
    ylo = tm // 2
    z = height % NZ
    yhi = height // NZ
    y = 2 * yhi + ylo

    def dev(x_, y_, z_, c_):
        return (x_, (y_ % 2) * 2 + c_, (y_ // 2) * NZ + z_)

    up_y, down_y = (y + 1) % 4, (y + 3) % 4
    up_z, down_z = (z + 1) % NZ, (z + NZ - 1) % NZ

    def remote(src, dst, ssem, rsem, target):
        return pltpu.make_async_remote_copy(
            src_ref=src, dst_ref=dst, send_sem=ssem, recv_sem=rsem,
            device_id=target, device_id_type=MESH,
        )

    y_own = 2 * (x // 2) + yhi
    z_own = 4 * (x % 2) + 2 * ylo
    x_src = 2 * (y // 2) + z // 4
    y_src = 2 * (y % 2) + (z % 4) // 2

    barrier = pltpu.get_barrier_semaphore()

    def greet(target):
        pl.semaphore_signal(barrier, inc=1, device_id=target, device_id_type=MESH)

    for d in range(1, 4):
        greet(dev(x, (y + d) % 4, z, c))
        greet(dev((x + d) % 4, y, z, c))
    greet(dev(x, y, z, 1 - c))
    for d in range(1, NZ):
        greet(dev(x, y, (z + d) % NZ, c))
    from_self = jnp.logical_and(x_src == x, y_src == y)
    for d in range(NZ):
        src_z = (z + d) % NZ
        if d == 0:
            @pl.when(jnp.logical_not(from_self))
            def _():
                greet(dev(x_src, y_src, z, c))
        else:
            greet(dev(x_src, y_src, src_z, c))
    pl.semaphore_wait(barrier, 22 - from_self.astype(jnp.int32))

    def slab(ref, y_, c_, f):
        return ref.at[2 * (2 * (y_ % 2) + c_) + f, y_ // 2]

    def block(ref, y_, c_):
        return ref.at[pl.ds(2 * (2 * (y_ % 2) + c_), 2), y_ // 2]

    arrays = ((og_in, og), (lat_in, xg))
    far = (y + 2) % 4

    def gather(n, i):
        src, ref = arrays[n]
        up, down, mate = dev(x, up_y, z, c), dev(x, down_y, z, c), dev(x, y, z, 1 - c)
        plan = {
            0: lambda: (src.at[0], slab(ref, y, c, 0), up),
            1: lambda: (src.at[1], slab(ref, y, c, 1), down),
            2: lambda: (src.at[1], slab(ref, y, c, 1), up),
            3: lambda: (src.at[0], slab(ref, y, c, 0), down),
            4: lambda: (src, block(ref, y, c), mate),
            5: lambda: (slab(ref, down_y, c, 0), slab(ref, down_y, c, 0), up),
            6: lambda: (slab(ref, up_y, c, 1), slab(ref, up_y, c, 1), down),
            7: lambda: (block(ref, down_y, c), block(ref, down_y, c), mate),
            8: lambda: (block(ref, up_y, c), block(ref, up_y, c), mate),
            9: lambda: (block(ref, far, c), block(ref, far, c), mate),
        }
        s, d, t = plan[i]()
        return remote(s, d, ag_s.at[n, i], ag_r.at[n, i], t)

    pos = (z + NZ - 4 * c) % NZ

    def right(k):
        s = (pos + NZ - k) % NZ
        slot = s % 4
        src = wt_in if k == 0 else w.at[:, :, slot]
        return s < 4, remote(src, w.at[:, :, slot], wr_s.at[k], wr_r.at[k], dev(x, y, up_z, c))

    def right_came(k):
        return (pos + 2 * NZ - k - 1) % NZ < 4

    def left(k):
        s = (pos + k) % NZ
        slot = s % 4
        src = wt_in if k == 0 else w.at[:, :, slot]
        return s < 4, remote(src, w.at[:, :, slot], wl_s.at[k], wl_r.at[k], dev(x, y, down_z, c))

    def left_came(k):
        return (pos + k + 1) % NZ < 4

    def start_if(pair):
        ok, copy = pair

        @pl.when(ok)
        def _():
            copy.start()

    def wait_recv_if(ok, copy):
        @pl.when(ok)
        def _():
            copy.wait_recv()

    def w_step(k):
        wait_recv_if(right_came(k), right(k)[1])
        if k < 3:
            start_if(right(k + 1))
            wait_recv_if(left_came(k), left(k)[1])
            if k < 2:
                start_if(left(k + 1))

    start_if(right(0))
    start_if(left(0))
    for i in range(5):
        gather(0, i).start()
    for i in range(5):
        gather(1, i).start()
    own = [
        pltpu.make_async_copy(og_in, block(og, y, c), loc_s.at[0]),
        pltpu.make_async_copy(lat_in, block(xg, y, c), loc_s.at[1]),
    ]
    own_w = pltpu.make_async_copy(wt_in, w.at[:, :, pos % 4], loc_s.at[2])
    for copy in own:
        copy.start()

    @pl.when(pos < 4)
    def _():
        own_w.start()

    w2_copies = []
    for a in range(3):
        for s in range(4):
            first = 32 * (yhi * NZ + 4 * c + s) + 16 * ylo
            w2_copies.append(pltpu.make_async_copy(
                w2_in.at[pl.ds(9 * a, 9), pl.ds(pl.multiple_of(first, 16), 16)],
                w2.at[:, a, s], w2_s.at[a, s],
            ))
    for copy in w2_copies:
        copy.start()

    acc[...] = jnp.zeros_like(acc)
    q[...] = jnp.zeros_like(q)
    gi[...] = jnp.zeros_like(gi)

    for n in range(2):
        gather(n, 0).wait_recv()
        gather(n, 5).start()
        gather(n, 1).wait_recv()
        gather(n, 6).start()
    w_step(0)
    for n in range(2):
        gather(n, 2).wait_recv()
        gather(n, 7).start()
        gather(n, 3).wait_recv()
        gather(n, 8).start()
    w_step(1)
    for n in range(2):
        gather(n, 5).wait_recv()
        gather(n, 6).wait_recv()
        gather(n, 9).start()
    w_step(2)
    own[0].wait()
    for i in (4, 7, 8, 9):
        gather(0, i).wait_recv()

    def sum_step(i, _):
        f, band = i // 2, i % 2
        part = dot(sums_in[...], og[f, band], NN)
        for k in range(9):
            g[k, f, band] = part[64 * k : 64 * k + 64].astype(BF)
        for k in range(6):
            gh[k, f, band] = part[576 + 16 * k : 592 + 16 * k].astype(BF)
        return 0

    lax.fori_loop(0, 16, sum_step, 0)

    for copy in w2_copies:
        copy.wait()

    def q_step(k, _):
        wk = w2[k].reshape(192, 256)
        q[...] += dot(g[k].reshape(1024, 256), wk, NT).reshape(8, 2, 64, 192)
        return 0

    lax.fori_loop(0, 9, q_step, 0)
    for side in range(2):
        total = None
        for e in range(3):
            wk = w2[6 * side + e].reshape(192, 256)
            term = dot(gh[3 * side + e].reshape(256, 256), wk, NT)
            total = term if total is None else total + term
        qh[side] = total.reshape(8, 2, 16, 192)

    def through_time(ref, t):
        out = ref[t, :, :, 128:192]
        if t < 7:
            out = out + ref[t + 1, :, :, 64:128]
        if t < 6:
            out = out + ref[t + 2, :, :, 0:64]
        return out

    for t in range(8):
        ga[t] = through_time(q, t)

    w_step(3)

    @pl.when(pos < 4)
    def _():
        own_w.wait()

    own[1].wait()
    for i in (4, 7, 8, 9):
        gather(1, i).wait_recv()

    for a in range(3):
        n = 6 + a
        for b in range(3):
            part = dot(xg[0:n].reshape(n * 128, 512), w[3 * a + b].reshape(192, 512), NT)
            acc[2 - a : 8, :, 16 * (2 - b) : 16 * (2 - b) + 64, :] += part.reshape(n, 2, 64, 192)

    col96 = lax.broadcasted_iota(jnp.int32, (192, 64), 0) % 16

    def columns(t, _):
        part = acc[t].reshape(192, 192)
        before = jnp.where(col96 == 0, 0.0, pltpu.roll(part[:, 0:64], 1, 0))
        after = jnp.where(col96 == 15, 0.0, pltpu.roll(part[:, 128:192], 191, 0))
        pre[t] = (before + part[:, 64:128] + after).reshape(2, 96, 64)
        return 0

    lax.fori_loop(0, 8, columns, 0)

    for t in range(8):
        for side in range(2):
            rim = pre[t, :, 80 * side : 80 * side + 16]
            e1s[side, t] = jnp.concatenate([rim, through_time(qh.at[side], t)], axis=-1).astype(BF)

    def edge_copy(src, dst, base, side):
        target = dev(x, y, down_z if side == 0 else up_z, c)
        return remote(src.at[side], dst.at[side], e_s.at[base, side], e_r.at[base, side], target)

    for side in range(2):
        edge_copy(e1s, e1r, 0, side).start()
    for side in range(2):
        edge_copy(e1s, e1r, 0, side).wait_recv()

    last, first = z == NZ - 1, z == 0

    def from_below(v):
        return jnp.where(last, jnp.stack([v[1], jnp.zeros_like(v[1])]), v)

    def from_above(v):
        return jnp.where(first, jnp.stack([jnp.zeros_like(v[0]), v[0]]), v)

    for t in range(8):
        below = from_below(e1r[0, t].astype(F32))
        above = from_above(e1r[1, t].astype(F32))
        zero = jnp.zeros((2, 32, 128), F32)
        both = jnp.concatenate([above, zero, below], axis=1)
        v = pre[t, :, 16:80] + both[:, :, 0:64]
        d = ga[t] + both[:, :, 64:128]
        s = 1.0 / (1.0 + jnp.exp(-v))
        a_now = v * s
        p_now = d * (s * (1.0 + v * (1.0 - s)))
        act[t] = a_now
        pre[t, :, 16:80] = p_now
        pair = jnp.concatenate([a_now, p_now], axis=-1).astype(BF)
        e2s[0, t] = pair[:, 0:16]
        e2s[1, t] = pair[:, 48:64]

    for side in range(2):
        edge_copy(e2s, e2r, 1, side).start()

    def stacked(ref, t):
        v = ref[t]
        zero = jnp.zeros_like(v)
        return jnp.concatenate([ref[t - 2] if t > 1 else zero, ref[t - 1] if t > 0 else zero, v], axis=-1)

    for t in range(8):
        act3[t] = stacked(act, t).astype(BF)
    act3t[...] = dot(eye_in[...], act3[...].reshape(1024, 192), NT).astype(BF)

    for side in range(2):
        edge_copy(e2s, e2r, 1, side).wait_recv()

    for t in range(8):
        below = from_below(e2r[0, t].astype(F32))
        above = from_above(e2r[1, t].astype(F32))
        pre[t, :, 0:16] = above[:, :, 64:128]
        pre[t, :, 80:96] = below[:, :, 64:128]
        qh[0, t, :, :, 0:64] = above[:, :, 0:64]
        qh[1, t, :, :, 0:64] = below[:, :, 0:64]
    for side in range(2):
        rows = []
        for t in range(8):
            v = qh[side, t, :, :, 0:64]
            zero = jnp.zeros_like(v)
            rows.append(jnp.concatenate([
                qh[side, t - 2, :, :, 0:64] if t > 1 else zero,
                qh[side, t - 1, :, :, 0:64] if t > 0 else zero, v], axis=-1).reshape(32, 192))
        stack = jnp.concatenate(rows, axis=0).astype(BF)
        hal3t[side] = dot(eye_in[...], stack, NT).astype(BF)

    for k in range(9):
        part = dot(act3t[...], g[k].reshape(1024, 256), NN)
        if k // 3 != 1:
            side = k // 6
            part = part + dot(hal3t[side], gh[3 * side + k % 3].reshape(256, 256), NN)
        gws[k] = part.astype(BF).reshape(3, 4, 16, 256)

    def x_copy(d):
        to = (x + d) % 4
        return remote(gws.at[:, :, to], ra.at[d - 1], a_s.at[d - 1], a_r.at[d - 1], dev(to, y, z, c))

    for d in range(1, 4):
        x_copy(d).start()

    def shifted(t, _):
        part = pre[t].reshape(192, 64)
        after = jnp.where(col96 == 15, 0.0, pltpu.roll(part, 191, 0))
        before = jnp.where(col96 == 0, 0.0, pltpu.roll(part, 1, 0))
        gp3[t] = jnp.concatenate([after, part, before], axis=-1).reshape(2, 96, 192).astype(BF)
        return 0

    lax.fori_loop(0, 8, shifted, 0)
    for a in range(3):
        n = 6 + a
        for b in range(3):
            rows = gp3[2 - a : 8, :, 16 * (2 - b) : 16 * (2 - b) + 64, :].reshape(n * 128, 192)
            part = dot(rows, w[3 * a + b].reshape(192, 512), NN)
            gi[0:n] += part.reshape(n, 2, 64, 512)

    for half in range(2):
        for f in range(2):
            pb[half, f] = gi[4 * half + 2 * (1 - c) + f].astype(BF)
    pair_copy = remote(pb, rp, pr_s, pr_r, dev(x, y, z, 1 - c))
    pair_copy.start()

    for d in range(1, 4):
        x_copy(d).wait_recv()

    def x_sum(k, _):
        total = gws[k, :, x].astype(F32)
        for d in range(3):
            total = total + ra[d, k].astype(F32)
        sb[pl.ds(3 * k, 3)] = total.astype(BF)
        return 0

    lax.fori_loop(0, 9, x_sum, 0)
    sb[27:32] = jnp.zeros((5, 16, 256), BF)

    def z_copy(d):
        to = (z + d) % NZ
        return remote(sb.at[pl.ds(4 * to, 4)], rb.at[d - 1], b_s.at[d - 1], b_r.at[d - 1], dev(x, y, to, c))

    for d in range(1, NZ):
        z_copy(d).start()

    pair_copy.wait_recv()
    for half in range(2):
        for f in range(2):
            ps[half, f] = (gi[4 * half + 2 * c + f] + rp[half, f].astype(F32)).astype(BF)

    def y_copy(d):
        to = (y + d) % 4
        return remote(ps.at[to % 2, :, to // 2], rr.at[d - 1], rs_s.at[d - 1], rs_r.at[d - 1], dev(x, to, z, c))

    for d in range(1, 4):
        y_copy(d).start()

    for d in range(1, NZ):
        z_copy(d).wait_recv()
    total = sb[pl.ds(4 * z, 4)].astype(F32)
    for d in range(NZ - 1):
        total = total + rb[d].astype(F32)
    fc[...] = (total * scale).reshape(4, 2, 8, 256)

    def out_copy(to_x, half):
        target = dev(to_x, y_own, z_own + half, c)
        return remote(fc.at[:, half], rc.at[z], c_s.at[to_x, half], c_r.at[z], target)

    def out_self(half):
        return pltpu.make_async_copy(fc.at[:, half], rc.at[z], c_r.at[z])

    for half in range(2):
        for to_x in range(4):
            mine = jnp.logical_and(jnp.logical_and(x == to_x, y == y_own), z == z_own + half)

            @pl.when(mine)
            def _():
                out_self(half).start()

            @pl.when(jnp.logical_not(mine))
            def _():
                out_copy(to_x, half).start()

    for d in range(1, 4):
        y_copy(d).wait_recv()
    total = ps[ylo, :, yhi].astype(F32)
    for d in range(3):
        total = total + rr[d].astype(F32)
    gi_out[...] = total.astype(BF)

    for s in range(NZ):
        pltpu.make_async_copy(rc.at[s], rc.at[s], c_r.at[s]).wait()
    gw_out[...] = rc[...].reshape(32, 8, 256)

    for n in range(2):
        for i in range(10):
            gather(n, i).wait_send()
    for k in range(4):
        ok, copy = right(k)

        @pl.when(ok)
        def _():
            copy.wait_send()
    for k in range(3):
        ok, copy = left(k)

        @pl.when(ok)
        def _():
            copy.wait_send()
    for side in range(2):
        edge_copy(e1s, e1r, 0, side).wait_send()
        edge_copy(e2s, e2r, 1, side).wait_send()
    pair_copy.wait_send()
    for d in range(1, 4):
        x_copy(d).wait_send()
        y_copy(d).wait_send()
    for d in range(1, NZ):
        z_copy(d).wait_send()
    for half in range(2):
        for to_x in range(4):
            mine = jnp.logical_and(jnp.logical_and(x == to_x, y == y_own), z == z_own + half)

            @pl.when(jnp.logical_not(mine))
            def _():
                out_copy(to_x, half).wait_send()


def on_device(latent, out_grad, w_first, w_second):
    ylo = lax.axis_index("tm") // 2
    half = lax.dynamic_slice_in_dim(w_first, 16 * ylo, 16, axis=2)
    wt = jnp.swapaxes(half, 1, 2).reshape(9, 3, 16, 512)
    scale = 1.0 / math.sqrt(131072.0)
    hbm = pl.BlockSpec(memory_space=pl.ANY)
    vmem = pl.BlockSpec(memory_space=pltpu.VMEM)
    dma = pltpu.SemaphoreType.DMA
    grad_input, grad_w2 = pl.pallas_call(
        functools.partial(body, scale),
        out_shape=(
            jax.ShapeDtypeStruct((2, 64, 512), BF),
            jax.ShapeDtypeStruct((32, 8, 256), F32),
        ),
        in_specs=[hbm, hbm, hbm, hbm, vmem, vmem],
        out_specs=(vmem, vmem),
        scratch_shapes=[
            pltpu.VMEM((8, 2, 64, 512), BF),
            pltpu.VMEM((8, 2, 256, 256), BF),
            pltpu.VMEM((9, 3, 4, 16, 512), BF),
            pltpu.VMEM((9, 3, 4, 16, 256), BF),
            pltpu.VMEM((9, 8, 2, 64, 256), BF),
            pltpu.VMEM((6, 8, 2, 16, 256), BF),
            pltpu.VMEM((8, 2, 96, 192), F32),
            pltpu.VMEM((8, 2, 64, 192), F32),
            pltpu.VMEM((2, 8, 2, 16, 192), F32),
            pltpu.VMEM((8, 2, 96, 64), F32),
            pltpu.VMEM((8, 2, 64, 64), F32),
            pltpu.VMEM((2, 8, 2, 16, 128), BF),
            pltpu.VMEM((2, 8, 2, 16, 128), BF),
            pltpu.VMEM((2, 8, 2, 16, 128), BF),
            pltpu.VMEM((2, 8, 2, 16, 128), BF),
            pltpu.VMEM((8, 2, 64, 64), F32),
            pltpu.VMEM((8, 2, 96, 192), BF),
            pltpu.VMEM((8, 2, 64, 192), BF),
            pltpu.VMEM((192, 1024), BF),
            pltpu.VMEM((2, 192, 256), BF),
            pltpu.VMEM((8, 2, 64, 512), F32),
            pltpu.VMEM((2, 2, 2, 64, 512), BF),
            pltpu.VMEM((2, 2, 2, 64, 512), BF),
            pltpu.VMEM((2, 2, 2, 64, 512), BF),
            pltpu.VMEM((3, 2, 64, 512), BF),
            pltpu.VMEM((9, 3, 4, 16, 256), BF),
            pltpu.VMEM((3, 9, 3, 16, 256), BF),
            pltpu.VMEM((32, 16, 256), BF),
            pltpu.VMEM((7, 4, 16, 256), BF),
            pltpu.VMEM((4, 2, 8, 256), F32),
            pltpu.VMEM((8, 4, 8, 256), F32),
            dma((2, 10)), dma((2, 10)),
            dma((4,)), dma((4,)), dma((3,)), dma((3,)),
            dma((3, 4)), dma((3,)),
            dma((2, 2)), dma((2, 2)),
            dma, dma,
            dma((3,)), dma((3,)),
            dma((3,)), dma((3,)),
            dma((7,)), dma((7,)),
            dma((4, 2)), dma((8,)),
        ],
        compiler_params=pltpu.CompilerParams(
            collective_id=0, has_side_effects=True, vmem_limit_bytes=56 * 1024 * 1024
        ),
    )(
        latent.reshape(2, 64, 512),
        out_grad.reshape(2, 256, 256),
        wt,
        w_second,
        jnp.asarray(cell_sums(), BF),
        jnp.asarray(np.eye(192, dtype=np.float32), BF),
    )
    grad_w2 = grad_w2[:27].reshape(9, 3, 8, 256).transpose(2, 1, 0, 3).reshape(8, 27, 256)
    return grad_input.reshape(1, 2, 4, 16, 512), grad_w2


def solution(mesh):
    placed = (
        P("dp", "tm", "height", None, None),
        P("dp", "tm", "height", None, None),
        P(None, None, "height"),
        P(),
    )
    return jax.shard_map(
        on_device,
        mesh=mesh,
        in_specs=placed,
        out_specs=(P("dp", "tm", "height", None, None), P(("tm", "height"), None, None)),
        check_vma=False,
    )
```

```python
import functools
import math

import jax
import jax.numpy as jnp
import numpy as np
from jax import lax
from jax.experimental import pallas as pl
from jax.experimental.pallas import tpu as pltpu
from jax.sharding import PartitionSpec as P

MESH = pl.DeviceIdType.MESH
BF = jnp.bfloat16
F32 = jnp.float32
NZ = 8
NT = (((1,), (1,)), ((), ()))
NN = (((1,), (0,)), ((), ()))


def cell_sums():
    main = np.zeros((3, 3, 4, 16, 8, 32), np.float32)
    edge = np.zeros((2, 3, 16, 8, 32), np.float32)
    for b in range(3):
        for e in range(3):
            for c in range(16):
                cols = [2 * c + q + 1 - e for q in range(2) if 0 <= 2 * c + q + 1 - e < 32]
                for h in range(4):
                    for p in range(2):
                        row = 2 * h + p + 1 - b
                        if 0 <= row < 8:
                            main[b, e, h, c, row, cols] = 1.0
                if b == 0:
                    edge[0, e, c, 0, cols] = 1.0
                if b == 2:
                    edge[1, e, c, 7, cols] = 1.0
    return np.concatenate([main.reshape(576, 256), edge.reshape(96, 256)], axis=0)


def dot(a, b, dims):
    return lax.dot_general(a, b, dims, preferred_element_type=F32)


def body(
    scale,
    lat_in, og_in, wt_in, w2_in, sums_in, eye_in,
    gi_out, gw_out,
    xg, og, w, w2, g, gh, acc, q, qh, pre, ga, es, er,
    act, gp3, act3, act3t, hal3t, gi, pb, rp, ps, rr, gws, ra, sbf, sb, rb, fc, rc,
    loc_s, ag_s, ag_r, wz_s, wz_r, wx_s, wx_r, e_s, e_r, pr_s, pr_r, rs_s, rs_r,
    a_s, a_r, b_s, b_r, c_s, c_r,
):
    x = lax.axis_index("dp")
    tm = lax.axis_index("tm")
    height = lax.axis_index("height")
    c = tm % 2
    ylo = tm // 2
    z = height % NZ
    yhi = height // NZ
    y = 2 * yhi + ylo
    y_out = 2 * ylo + yhi

    def dev(x_, y_, z_, c_):
        return (x_, (y_ % 2) * 2 + c_, (y_ // 2) * NZ + z_)

    up_y, down_y = (y + 1) % 4, (y + 3) % 4
    up_z, down_z = (z + 1) % NZ, (z + NZ - 1) % NZ
    up_x, down_x = (x + 1) % 4, (x + 3) % 4
    far_y, far_x = (y + 2) % 4, (x + 2) % 4

    def remote(src, dst, ssem, rsem, target):
        return pltpu.make_async_remote_copy(
            src_ref=src, dst_ref=dst, send_sem=ssem, recv_sem=rsem,
            device_id=target, device_id_type=MESH,
        )

    def slab(ref, y_, c_, f):
        return ref.at[2 * (2 * (y_ % 2) + c_) + f, y_ // 2]

    def block(ref, y_, c_):
        return ref.at[pl.ds(2 * (2 * (y_ % 2) + c_), 2), y_ // 2]

    pos = (z + NZ - (4 * c + 2 * ylo)) % NZ
    source = pos < 2
    base = 64 * (4 * yhi + 2 * c + ylo)
    own = [
        pltpu.make_async_copy(lat_in, block(xg, y, c), loc_s.at[0]),
        pltpu.make_async_copy(og_in, block(og, y, c), loc_s.at[1]),
    ]
    own_w = pltpu.make_async_copy(wt_in, w.at[:, pos % 2], loc_s.at[2])
    w2_copies = [
        pltpu.make_async_copy(
            w2_in.at[pl.ds(9 * a, 9), pl.ds(pl.multiple_of(base, 64), 64)], w2.at[:, a], loc_s.at[3 + a]
        )
        for a in range(3)
    ]

    @pl.when(source)
    def _():
        own_w.start()

    for copy in own:
        copy.start()

    barrier = pltpu.get_barrier_semaphore()

    def greet(target):
        pl.semaphore_signal(barrier, inc=1, device_id=target, device_id_type=MESH)

    greet(dev(x, y, z, 1 - c))
    for d in (1, 3, 2):
        greet(dev(x, (y + d) % 4, z, c))
        greet(dev((x + d) % 4, y, z, c))
    for d in (1, 7, 2, 6, 3, 5, 4):
        greet(dev(x, y, (z + d) % NZ, c))
    swaps = y != y_out

    @pl.when(swaps)
    def _():
        for d in range(1, 4):
            greet(dev((x + d) % 4, y_out, z, c))

    for copy in w2_copies:
        copy.start()
    acc[...] = jnp.zeros_like(acc)

    @pl.when(source)
    def _():
        own_w.wait()

    for copy in own:
        copy.wait()
    pl.semaphore_wait(barrier, 14 + 3 * swaps.astype(jnp.int32))

    arrays = (xg, og)

    def gather(n, i):
        ref = arrays[n]
        up, down, mate = dev(x, up_y, z, c), dev(x, down_y, z, c), dev(x, y, z, 1 - c)
        place, target = {
            0: lambda: (slab(ref, y, c, 0), up),
            1: lambda: (slab(ref, y, c, 1), down),
            2: lambda: (slab(ref, y, c, 1), up),
            3: lambda: (slab(ref, y, c, 0), down),
            4: lambda: (block(ref, y, c), mate),
            5: lambda: (slab(ref, down_y, c, 0), up),
            6: lambda: (slab(ref, up_y, c, 1), down),
            7: lambda: (block(ref, down_y, c), mate),
            8: lambda: (block(ref, up_y, c), mate),
            9: lambda: (block(ref, far_y, c), mate),
        }[i]()
        return remote(place, place, ag_s.at[n, i], ag_r.at[n, i], target)

    reach = (4, 3)

    def share(part, slot):
        if part == 0:
            return w.at[pl.ds(4 * x, 4), slot]
        return w.at[16:27, slot]

    def along_z(part, slot, way):
        target = dev(x, y, up_z if way == 0 else down_z, c)
        place = share(part, slot)
        return remote(place, place, wz_s.at[part, slot, way], wz_r.at[part, slot], target)

    def z_sends(part, slot, act_on):
        far = (pos + NZ - slot) % NZ
        r = reach[part]

        @pl.when(far < r)
        def _():
            act_on(along_z(part, slot, 0))

        @pl.when(jnp.logical_or(far == 0, far > r + 1))
        def _():
            act_on(along_z(part, slot, 1))

    def z_recv(part, slot):
        @pl.when(pos != slot)
        def _():
            along_z(part, slot, 0).wait_recv()

    def along_x(slot, i):
        up, down = dev(up_x, y, z, c), dev(down_x, y, z, c)
        first, target = {
            0: lambda: (4 * x, up),
            1: lambda: (4 * x, down),
            2: lambda: (4 * down_x, up),
            3: lambda: (4 * up_x + 2, down),
        }[i]()
        place = w.at[pl.ds(first, 4 if i < 2 else 2), slot]
        return remote(place, place, wx_s.at[slot, i], wx_r.at[slot, i], target)

    def start(copy):
        copy.start()

    near = jnp.where(jnp.logical_and(pos >= 1, pos <= 4), 1, 0)
    slots = (near, 1 - near)
    own_slot = pos % 2

    @pl.when(source)
    def _():
        z_sends(0, own_slot, start)

    for i in range(5):
        gather(0, i).start()

    @pl.when(source)
    def _():
        z_sends(1, own_slot, start)

    for i in range(5):
        gather(1, i).start()

    def pass_on(part, slot):
        @pl.when(pos != slot)
        def _():
            along_z(part, slot, 0).wait_recv()
            z_sends(part, slot, start)
            if part == 0:
                along_x(slot, 0).start()
                along_x(slot, 1).start()

    def pass_x(slot):
        @pl.when(pos != slot)
        def _():
            along_x(slot, 0).wait_recv()
            along_x(slot, 2).start()
            along_x(slot, 1).wait_recv()
            along_x(slot, 3).start()

    def pass_y(n):
        gather(n, 0).wait_recv()
        gather(n, 5).start()
        gather(n, 1).wait_recv()
        gather(n, 6).start()

    def pass_mate(n):
        gather(n, 2).wait_recv()
        gather(n, 7).start()
        gather(n, 3).wait_recv()
        gather(n, 8).start()

    def pass_far(n):
        gather(n, 5).wait_recv()
        gather(n, 6).wait_recv()
        gather(n, 9).start()

    pass_on(0, slots[0])
    pass_y(0)
    pass_on(0, slots[1])
    pass_mate(0)
    pass_x(slots[0])
    pass_on(1, slots[0])
    pass_y(1)
    pass_far(0)
    pass_x(slots[1])
    pass_on(1, slots[1])
    pass_mate(1)
    pass_far(1)

    for i in (4, 7, 8, 9):
        gather(0, i).wait_recv()
    for slot in range(2):
        @pl.when(pos != slot)
        def _():
            along_x(slot, 2).wait_recv()
            along_x(slot, 3).wait_recv()

    for a in range(3):
        n = 6 + a
        for b in range(3):
            k = 9 * a + 3 * b
            part = dot(xg[0:n].reshape(n * 128, 512), w[k : k + 3].reshape(192, 512), NT)
            acc[2 - a : 8, :, 16 * (2 - b) : 16 * (2 - b) + 64, :] += part.reshape(n, 2, 64, 192)

    col96 = lax.broadcasted_iota(jnp.int32, (192, 64), 0) % 16

    def columns(t, _):
        part = acc[t].reshape(192, 192)
        before = jnp.where(col96 == 0, 0.0, pltpu.roll(part[:, 0:64], 1, 0))
        after = jnp.where(col96 == 15, 0.0, pltpu.roll(part[:, 128:192], 191, 0))
        pre[t] = (before + part[:, 64:128] + after).reshape(2, 96, 64)
        return 0

    lax.fori_loop(0, 8, columns, 0)

    def edge_copy(n, side):
        target = dev(x, y, down_z if side == 0 else up_z, c)
        return remote(es.at[n, side], er.at[n, side], e_s.at[n, side], e_r.at[n, side], target)

    def edge_send(n, rows):
        for side in range(2):
            for t in range(4):
                es[n, side, t] = jnp.concatenate([rows(side, t), rows(side, t + 4)], axis=-1).astype(BF)
            edge_copy(n, side).start()

    def edge_wait(n):
        for side in range(2):
            edge_copy(n, side).wait_recv()

    last, first = z == NZ - 1, z == 0

    def edge_rows(n, side, t):
        v = er[n, side, t % 4][:, :, 64 * (t // 4) : 64 * (t // 4) + 64].astype(F32)
        if side == 0:
            return jnp.where(last, jnp.stack([v[1], jnp.zeros_like(v[1])]), v)
        return jnp.where(first, jnp.stack([jnp.zeros_like(v[0]), v[0]]), v)

    edge_send(0, lambda side, t: pre[t, :, 80 * side : 80 * side + 16])

    for i in (4, 7, 8, 9):
        gather(1, i).wait_recv()

    def sum_step(i, _):
        f, band = i // 2, i % 2
        part = dot(sums_in[...], og[f, band], NN)
        for k in range(9):
            g[k, f, band] = part[64 * k : 64 * k + 64].astype(BF)
        for k in range(6):
            gh[k, f, band] = part[576 + 16 * k : 592 + 16 * k].astype(BF)
        return 0

    lax.fori_loop(0, 16, sum_step, 0)
    for copy in w2_copies:
        copy.wait()
    q[...] = jnp.zeros_like(q)

    def q_step(k, _):
        wk = w2[k].reshape(192, 256)
        q[...] += dot(g[k].reshape(1024, 256), wk, NT).reshape(8, 2, 64, 192)
        return 0

    lax.fori_loop(0, 9, q_step, 0)
    for side in range(2):
        total = None
        for e in range(3):
            wk = w2[6 * side + e].reshape(192, 256)
            term = dot(gh[3 * side + e].reshape(256, 256), wk, NT)
            total = term if total is None else total + term
        qh[side] = total.reshape(8, 2, 16, 192)

    def through_time(ref, t):
        out = ref[t, :, :, 128:192]
        if t < 7:
            out = out + ref[t + 1, :, :, 64:128]
        if t < 6:
            out = out + ref[t + 2, :, :, 0:64]
        return out

    edge_send(1, lambda side, t: through_time(qh.at[side], t))
    for t in range(8):
        ga[t] = through_time(q, t)

    edge_wait(0)
    for t in range(8):
        pre[t, :, 16:32] += edge_rows(0, 1, t)
        pre[t, :, 64:80] += edge_rows(0, 0, t)
        v = pre[t, :, 16:80]
        s = 1.0 / (1.0 + jnp.exp(-v))
        act[t] = v * s
        pre[t, :, 16:80] = s * (1.0 + v * (1.0 - s))
    edge_send(2, lambda side, t: act[t, :, 48 * side : 48 * side + 16])

    def stacked(rows, t):
        v = rows(t)
        zero = jnp.zeros_like(v)
        return jnp.concatenate([rows(t - 2) if t > 1 else zero, rows(t - 1) if t > 0 else zero, v], axis=-1)

    for t in range(8):
        act3[t] = stacked(lambda u: act[u], t).astype(BF)
    act3t[...] = dot(eye_in[...], act3[...].reshape(1024, 192), NT).astype(BF)

    edge_wait(1)
    for t in range(8):
        ga[t, :, 0:16] += edge_rows(1, 1, t)
        ga[t, :, 48:64] += edge_rows(1, 0, t)
        pre[t, :, 16:80] = ga[t] * pre[t, :, 16:80]
    edge_send(3, lambda side, t: pre[t, :, 16 + 48 * side : 32 + 48 * side])

    edge_wait(2)
    for t in range(8):
        for side in range(2):
            qh[side, t, :, :, 0:64] = edge_rows(2, 1 - side, t)
    for side in range(2):
        stack = jnp.concatenate(
            [stacked(lambda u: qh[side, u, :, :, 0:64], t).reshape(32, 192) for t in range(8)], axis=0
        ).astype(BF)
        hal3t[side] = dot(eye_in[...], stack, NT).astype(BF)

    for k in range(9):
        part = dot(act3t[...], g[k].reshape(1024, 256), NN)
        if k // 3 != 1:
            side = k // 6
            part = part + dot(hal3t[side], gh[3 * side + k % 3].reshape(256, 256), NN)
        gws[3 * k : 3 * k + 3] = part.astype(BF).reshape(3, 64, 256)
    gws[27] = jnp.zeros((64, 256), BF)

    def x_copy(d):
        to = (x + d) % 4
        return remote(gws.at[pl.ds(7 * to, 7)], ra.at[d - 1], a_s.at[d - 1], a_r.at[d - 1], dev(to, y, z, c))

    for d in (2, 1, 3):
        x_copy(d).start()

    edge_wait(3)
    for t in range(8):
        pre[t, :, 0:16] = edge_rows(3, 1, t)
        pre[t, :, 80:96] = edge_rows(3, 0, t)

    def shifted(t, _):
        part = pre[t].reshape(192, 64)
        after = jnp.where(col96 == 15, 0.0, pltpu.roll(part, 191, 0))
        before = jnp.where(col96 == 0, 0.0, pltpu.roll(part, 1, 0))
        gp3[t] = jnp.concatenate([after, part, before], axis=-1).reshape(2, 96, 192).astype(BF)
        return 0

    lax.fori_loop(0, 8, shifted, 0)
    gi[...] = jnp.zeros_like(gi)
    for a in range(3):
        n = 6 + a
        for b in range(3):
            k = 9 * a + 3 * b
            rows = gp3[2 - a : 8, :, 16 * (2 - b) : 16 * (2 - b) + 64, :].reshape(n * 128, 192)
            part = dot(rows, w[k : k + 3].reshape(192, 512), NN)
            gi[0:n] += part.reshape(n, 2, 64, 512)

    for half in range(2):
        for f in range(2):
            pb[half, f] = gi[4 * half + 2 * (1 - c) + f].astype(BF)
    pair_copy = remote(pb, rp, pr_s, pr_r, dev(x, y, z, 1 - c))
    pair_copy.start()

    for d in range(1, 4):
        x_copy(d).wait_recv()

    def x_sum(j, _):
        total = gws[7 * x + j].astype(F32)
        for d in range(3):
            total = total + ra[d, j].astype(F32)
        sbf[:, pl.ds(pl.multiple_of(8 * j, 8), 8)] = total.reshape(8, 8, 256)
        return 0

    lax.fori_loop(0, 7, x_sum, 0)
    sbf[:, 56:64] = jnp.zeros((8, 8, 256), F32)
    sb[...] = sbf[...].astype(BF)

    def z_copy(d):
        to = (z + d) % NZ
        return remote(sb.at[to], rb.at[d - 1], b_s.at[d - 1], b_r.at[d - 1], dev(x, y, to, c))

    for d in (4, 3, 5, 2, 6, 1, 7):
        z_copy(d).start()

    pair_copy.wait_recv()
    for half in range(2):
        for f in range(2):
            ps[half, f] = (gi[4 * half + 2 * c + f] + rp[half, f].astype(F32)).astype(BF)

    def y_copy(d):
        to = (y + d) % 4
        return remote(ps.at[to % 2, :, to // 2], rr.at[d - 1], rs_s.at[d - 1], rs_r.at[d - 1], dev(x, to, z, c))

    for d in (2, 1, 3):
        y_copy(d).start()

    for d in range(1, NZ):
        z_copy(d).wait_recv()
    total = sb[z].astype(F32)
    for d in range(NZ - 1):
        total = total + rb[d].astype(F32)
    fc[...] = (total * scale).astype(BF)

    def out_copy(to_x):
        return remote(fc, rc.at[x], c_s.at[to_x], c_r.at[x], dev(to_x, y_out, z, c))

    for to_x in range(4):
        mine = jnp.logical_and(x == to_x, y == y_out)

        @pl.when(mine)
        def _():
            pltpu.make_async_copy(fc, rc.at[x], c_r.at[x]).start()

        @pl.when(jnp.logical_not(mine))
        def _():
            out_copy(to_x).start()

    for d in range(1, 4):
        y_copy(d).wait_recv()
    total = ps[ylo, :, yhi].astype(F32)
    for d in range(3):
        total = total + rr[d].astype(F32)
    gi_out[...] = total.astype(BF)

    for part in range(4):
        pltpu.make_async_copy(fc, rc.at[part], c_r.at[part]).wait()
        v = rc[part].astype(F32)
        for j in range(7):
            k, a = (7 * part + j) // 3, (7 * part + j) % 3
            if k < 9:
                gw_out[9 * a + k] = v[8 * j : 8 * j + 8]

    def sent(copy):
        copy.wait_send()

    for n in range(2):
        for i in range(10):
            gather(n, i).wait_send()
        for slot in range(2):
            z_sends(n, slot, sent)
    for slot in range(2):
        @pl.when(pos != slot)
        def _():
            for i in range(4):
                along_x(slot, i).wait_send()

    for n in range(4):
        for side in range(2):
            edge_copy(n, side).wait_send()
    pair_copy.wait_send()
    for d in range(1, 4):
        x_copy(d).wait_send()
        y_copy(d).wait_send()
    for d in range(1, NZ):
        z_copy(d).wait_send()
    for to_x in range(4):
        @pl.when(jnp.logical_not(jnp.logical_and(x == to_x, y == y_out)))
        def _():
            out_copy(to_x).wait_send()


def on_device(latent, out_grad, w_first, w_second):
    wt = jnp.swapaxes(w_first, 1, 2)
    scale = 1.0 / math.sqrt(131072.0)
    hbm = pl.BlockSpec(memory_space=pl.ANY)
    vmem = pl.BlockSpec(memory_space=pltpu.VMEM)
    dma = pltpu.SemaphoreType.DMA
    grad_input, grad_w2 = pl.pallas_call(
        functools.partial(body, scale),
        out_shape=(
            jax.ShapeDtypeStruct((2, 64, 512), BF),
            jax.ShapeDtypeStruct((27, 8, 256), F32),
        ),
        in_specs=[hbm, hbm, hbm, hbm, vmem, vmem],
        out_specs=(vmem, vmem),
        scratch_shapes=[
            pltpu.VMEM((8, 2, 64, 512), BF),
            pltpu.VMEM((8, 2, 256, 256), BF),
            pltpu.VMEM((27, 2, 32, 512), BF),
            pltpu.VMEM((9, 3, 64, 256), BF),
            pltpu.VMEM((9, 8, 2, 64, 256), BF),
            pltpu.VMEM((6, 8, 2, 16, 256), BF),
            pltpu.VMEM((8, 2, 96, 192), F32),
            pltpu.VMEM((8, 2, 64, 192), F32),
            pltpu.VMEM((2, 8, 2, 16, 192), F32),
            pltpu.VMEM((8, 2, 96, 64), F32),
            pltpu.VMEM((8, 2, 64, 64), F32),
            pltpu.VMEM((4, 2, 4, 2, 16, 128), BF),
            pltpu.VMEM((4, 2, 4, 2, 16, 128), BF),
            pltpu.VMEM((8, 2, 64, 64), F32),
            pltpu.VMEM((8, 2, 96, 192), BF),
            pltpu.VMEM((8, 2, 64, 192), BF),
            pltpu.VMEM((192, 1024), BF),
            pltpu.VMEM((2, 192, 256), BF),
            pltpu.VMEM((8, 2, 64, 512), F32),
            pltpu.VMEM((2, 2, 2, 64, 512), BF),
            pltpu.VMEM((2, 2, 2, 64, 512), BF),
            pltpu.VMEM((2, 2, 2, 64, 512), BF),
            pltpu.VMEM((3, 2, 64, 512), BF),
            pltpu.VMEM((28, 64, 256), BF),
            pltpu.VMEM((3, 7, 64, 256), BF),
            pltpu.VMEM((8, 64, 256), F32),
            pltpu.VMEM((8, 64, 256), BF),
            pltpu.VMEM((7, 64, 256), BF),
            pltpu.VMEM((64, 256), BF),
            pltpu.VMEM((4, 64, 256), BF),
            dma((6,)),
            dma((2, 10)), dma((2, 10)),
            dma((2, 2, 2)), dma((2, 2)),
            dma((2, 4)), dma((2, 4)),
            dma((4, 2)), dma((4, 2)),
            dma, dma,
            dma((3,)), dma((3,)),
            dma((3,)), dma((3,)),
            dma((7,)), dma((7,)),
            dma((4,)), dma((4,)),
        ],
        compiler_params=pltpu.CompilerParams(
            collective_id=0, has_side_effects=True, vmem_limit_bytes=56 * 1024 * 1024
        ),
    )(
        latent.reshape(2, 64, 512),
        out_grad.reshape(2, 256, 256),
        wt,
        w_second,
        jnp.asarray(cell_sums(), BF),
        jnp.asarray(np.eye(192, dtype=np.float32), BF),
    )
    return grad_input.reshape(1, 2, 4, 16, 512), jnp.swapaxes(grad_w2, 0, 1)


def solution(mesh):
    placed = (
        P("dp", "tm", "height", None, None),
        P("dp", "tm", "height", None, None),
        P(None, None, "height"),
        P(),
    )
    return jax.shard_map(
        on_device,
        mesh=mesh,
        in_specs=placed,
        out_specs=(P("dp", "tm", "height", None, None), P(("tm", "height"), None, None)),
        check_vma=False,
    )
```

```python
import functools
import math

import jax
import jax.numpy as jnp
import numpy as np
from jax import lax
from jax.experimental import pallas as pl
from jax.experimental.pallas import tpu as pltpu
from jax.sharding import PartitionSpec as P

MESH = pl.DeviceIdType.MESH
BF = jnp.bfloat16
F32 = jnp.float32
NZ = 8
NT = (((1,), (1,)), ((), ()))
NN = (((1,), (0,)), ((), ()))


def cell_sums():
    main = np.zeros((3, 3, 4, 16, 8, 32), np.float32)
    edge = np.zeros((2, 3, 16, 8, 32), np.float32)
    for b in range(3):
        for e in range(3):
            for c in range(16):
                cols = [2 * c + q + 1 - e for q in range(2) if 0 <= 2 * c + q + 1 - e < 32]
                for h in range(4):
                    for p in range(2):
                        row = 2 * h + p + 1 - b
                        if 0 <= row < 8:
                            main[b, e, h, c, row, cols] = 1.0
                if b == 0:
                    edge[0, e, c, 0, cols] = 1.0
                if b == 2:
                    edge[1, e, c, 7, cols] = 1.0
    return np.concatenate([main.reshape(576, 256), edge.reshape(96, 256)], axis=0)


def dot(a, b, dims):
    return lax.dot_general(a, b, dims, preferred_element_type=F32)


def body(
    scale,
    lat_in, og_in, wt_in, w2_in, sums_in, eye_in,
    gi_out, gw_out,
    xg, og, w, w2, g, gh, acc, ah, q, qh, pre, ga, es, er,
    act, gp3, act3, act3t, hal3t, gi, pb, rp, ps, rr, gws, ra, sbf, sb, rb, fc, rc,
    loc_s, w2_s, ag_s, ag_r, wz_s, wz_r, wx_s, wx_r, e_s, e_r, pr_s, pr_r, rs_s, rs_r,
    a_s, a_r, b_s, b_r, c_s, c_r,
):
    x = lax.axis_index("dp")
    tm = lax.axis_index("tm")
    height = lax.axis_index("height")
    c = tm % 2
    ylo = tm // 2
    z = height % NZ
    yhi = height // NZ
    y = 2 * yhi + ylo
    y_out = 2 * ylo + yhi

    def dev(x_, y_, z_, c_):
        return (x_, (y_ % 2) * 2 + c_, (y_ // 2) * NZ + z_)

    up_y, down_y = (y + 1) % 4, (y + 3) % 4
    up_z, down_z = (z + 1) % NZ, (z + NZ - 1) % NZ
    up_x, down_x = (x + 1) % 4, (x + 3) % 4
    far_y, far_x = (y + 2) % 4, (x + 2) % 4

    def remote(src, dst, ssem, rsem, target):
        return pltpu.make_async_remote_copy(
            src_ref=src, dst_ref=dst, send_sem=ssem, recv_sem=rsem,
            device_id=target, device_id_type=MESH,
        )

    def slab(ref, y_, c_, f):
        return ref.at[2 * (2 * (y_ % 2) + c_) + f, y_ // 2]

    def block(ref, y_, c_):
        return ref.at[pl.ds(2 * (2 * (y_ % 2) + c_), 2), y_ // 2]

    pos = (z + NZ - (4 * c + 2 * ylo)) % NZ
    source = pos < 2
    base = 64 * (4 * yhi + 2 * c + ylo)
    own = [
        pltpu.make_async_copy(lat_in, block(xg, y, c), loc_s.at[0]),
        pltpu.make_async_copy(og_in, block(og, y, c), loc_s.at[1]),
    ]
    own_w = pltpu.make_async_copy(wt_in, w.at[:, pos % 2], loc_s.at[2])
    w2_copies = [
        pltpu.make_async_copy(
            w2_in.at[9 * a + k, pl.ds(pl.multiple_of(base, 64), 64)],
            w2.at[64 * a : 64 * a + 64, 256 * k : 256 * k + 256],
            w2_s.at[a, k],
        )
        for a in range(3)
        for k in range(9)
    ]

    @pl.when(source)
    def _():
        own_w.start()

    for copy in own:
        copy.start()

    barrier = pltpu.get_barrier_semaphore()

    def greet(target):
        pl.semaphore_signal(barrier, inc=1, device_id=target, device_id_type=MESH)

    greet(dev(x, y, z, 1 - c))
    for d in (1, 3, 2):
        greet(dev(x, (y + d) % 4, z, c))
        greet(dev((x + d) % 4, y, z, c))
    for d in (1, 7, 2, 6, 3, 5, 4):
        greet(dev(x, y, (z + d) % NZ, c))
    swaps = y != y_out

    @pl.when(swaps)
    def _():
        for d in range(1, 4):
            greet(dev((x + d) % 4, y_out, z, c))

    for copy in w2_copies:
        copy.start()
    acc[...] = jnp.zeros_like(acc)
    ah[...] = jnp.zeros_like(ah)

    @pl.when(source)
    def _():
        own_w.wait()

    for copy in own:
        copy.wait()
    pl.semaphore_wait(barrier, 14 + 3 * swaps.astype(jnp.int32))

    arrays = (og, xg)

    def gather(n, i):
        ref = arrays[n]
        up, down, mate = dev(x, up_y, z, c), dev(x, down_y, z, c), dev(x, y, z, 1 - c)
        place, target = {
            0: lambda: (slab(ref, y, c, 0), up),
            1: lambda: (slab(ref, y, c, 1), down),
            2: lambda: (slab(ref, y, c, 1), up),
            3: lambda: (slab(ref, y, c, 0), down),
            4: lambda: (block(ref, y, c), mate),
            5: lambda: (slab(ref, down_y, c, 0), up),
            6: lambda: (slab(ref, up_y, c, 1), down),
            7: lambda: (block(ref, down_y, c), mate),
            8: lambda: (block(ref, up_y, c), mate),
            9: lambda: (block(ref, far_y, c), mate),
        }[i]()
        return remote(place, place, ag_s.at[n, i], ag_r.at[n, i], target)

    reach = (4, 3, 3, 3)
    cuts = (0, 16, 20, 24, 27)

    def share(part, slot):
        if part == 0:
            return w.at[pl.ds(4 * x, 4), slot]
        return w.at[cuts[part] : cuts[part + 1], slot]

    def along_z(part, slot, way):
        target = dev(x, y, up_z if way == 0 else down_z, c)
        place = share(part, slot)
        return remote(place, place, wz_s.at[part, slot, way], wz_r.at[part, slot], target)

    def z_sends(part, slot, act_on):
        far = (pos + NZ - slot) % NZ
        r = reach[part]

        @pl.when(far < r)
        def _():
            act_on(along_z(part, slot, 0))

        @pl.when(jnp.logical_or(far == 0, far > r + 1))
        def _():
            act_on(along_z(part, slot, 1))

    def goes_on(part, slot):
        far = (pos + NZ - slot) % NZ
        r = reach[part]
        return jnp.logical_and(far != 0, jnp.logical_or(far < r, far > r + 1))

    def along_x(slot, i):
        up, down = dev(up_x, y, z, c), dev(down_x, y, z, c)
        first, target = {
            0: lambda: (4 * x, up),
            1: lambda: (4 * x, down),
            2: lambda: (4 * down_x, up),
            3: lambda: (4 * up_x + 2, down),
        }[i]()
        place = w.at[pl.ds(first, 4 if i < 2 else 2), slot]
        return remote(place, place, wx_s.at[slot, i], wx_r.at[slot, i], target)

    def start(copy):
        copy.start()

    closer = jnp.where(jnp.logical_and(pos >= 1, pos <= 4), 1, 0)
    slots = (closer, 1 - closer)
    own_slot = pos % 2

    @pl.when(source)
    def _():
        z_sends(0, own_slot, start)

    for i in range(5):
        gather(0, i).start()

    @pl.when(source)
    def _():
        z_sends(1, own_slot, start)
        z_sends(2, own_slot, start)
        z_sends(3, own_slot, start)

    for i in range(5):
        gather(1, i).start()

    def pass_on(part, slot):
        @pl.when(pos != slot if part == 0 else goes_on(part, slot))
        def _():
            along_z(part, slot, 0).wait_recv()
            z_sends(part, slot, start)
            if part == 0:
                along_x(slot, 0).start()
                along_x(slot, 1).start()

    def pass_end(part, slot):
        @pl.when(jnp.logical_and(pos != slot, jnp.logical_not(goes_on(part, slot))))
        def _():
            along_z(part, slot, 0).wait_recv()

    def pass_x(slot):
        @pl.when(pos != slot)
        def _():
            along_x(slot, 0).wait_recv()
            along_x(slot, 2).start()
            along_x(slot, 1).wait_recv()
            along_x(slot, 3).start()

    def pass_y(n):
        gather(n, 0).wait_recv()
        gather(n, 5).start()
        gather(n, 1).wait_recv()
        gather(n, 6).start()

    def pass_mate(n):
        gather(n, 2).wait_recv()
        gather(n, 7).start()
        gather(n, 3).wait_recv()
        gather(n, 8).start()

    def pass_far(n):
        gather(n, 5).wait_recv()
        gather(n, 6).wait_recv()
        gather(n, 9).start()

    near, far = slots
    pass_on(0, near)
    pass_y(0)
    pass_on(1, near)
    pass_on(0, far)
    pass_mate(0)
    pass_on(2, near)
    pass_on(1, far)
    pass_x(near)
    pass_y(1)
    pass_far(0)
    pass_on(3, near)
    pass_on(2, far)
    pass_mate(1)
    pass_far(1)

    for i in (4, 7, 8, 9):
        gather(0, i).wait_recv()

    def sums_of(f, band):
        part = dot(sums_in[...], og[f, band], NN)
        for k in range(9):
            g[f, band, :, 256 * k : 256 * k + 256] = part[64 * k : 64 * k + 64].astype(BF)
        for k in range(6):
            lane = 256 * (k % 3)
            gh[k // 3, f, band, :, lane : lane + 256] = part[576 + 16 * k : 592 + 16 * k].astype(BF)

    def sum_step(f, _):
        sums_of(f, 0)
        sums_of(f, 1)
        return 0

    lax.fori_loop(0, 4, sum_step, 0)
    pass_x(far)
    pass_on(3, far)
    lax.fori_loop(4, 8, sum_step, 0)
    for copy in w2_copies:
        copy.wait()

    def edge_copy(n, side):
        target = dev(x, y, down_z if side == 0 else up_z, c)
        return remote(es.at[n, side], er.at[n, side], e_s.at[n, side], e_r.at[n, side], target)

    def edge_send(n, rows):
        for side in range(2):
            for t in range(4):
                es[n, side, t] = jnp.concatenate([rows(side, t), rows(side, t + 4)], axis=-1).astype(BF)
            edge_copy(n, side).start()

    def edge_wait(n):
        for side in range(2):
            edge_copy(n, side).wait_recv()

    last, first = z == NZ - 1, z == 0

    def edge_rows(n, side, t):
        v = er[n, side, t % 4][:, :, 64 * (t // 4) : 64 * (t // 4) + 64].astype(F32)
        if side == 0:
            return jnp.where(last, jnp.stack([v[1], jnp.zeros_like(v[1])]), v)
        return jnp.where(first, jnp.stack([jnp.zeros_like(v[0]), v[0]]), v)

    def through_time(ref, t):
        out = ref[t, :, :, 128:192]
        if t < 7:
            out = out + ref[t + 1, :, :, 64:128]
        if t < 6:
            out = out + ref[t + 2, :, :, 0:64]
        return out

    for side in range(2):
        lanes = slice(1536 * side, 1536 * side + 768)
        qh[side] = dot(gh[side].reshape(256, 768), w2[:, lanes], NT).reshape(8, 2, 16, 192)
    edge_send(1, lambda side, t: through_time(qh.at[side], t))
    q[...] = dot(g[...].reshape(1024, 2304), w2[...], NT).reshape(8, 2, 64, 192)
    for t in range(8):
        ga[t] = through_time(q, t)

    for i in (4, 7, 8, 9):
        gather(1, i).wait_recv()
    for slot in range(2):
        for part in range(1, 4):
            pass_end(part, slot)

        @pl.when(pos != slot)
        def _():
            along_x(slot, 2).wait_recv()
            along_x(slot, 3).wait_recv()

    def summed_columns(part):
        rows = part.shape[0]
        col = lax.broadcasted_iota(jnp.int32, (rows, 64), 0) % 16
        before = jnp.where(col == 0, 0.0, pltpu.roll(part[:, 0:64], 1, 0))
        after = jnp.where(col == 15, 0.0, pltpu.roll(part[:, 128:192], rows - 1, 0))
        return before + part[:, 64:128] + after

    for side in range(2):
        for a in range(3):
            n = 6 + a
            k = 9 * a + 6 * (1 - side)
            rows = xg[0:n, :, 48 * side : 48 * side + 16].reshape(n * 32, 512)
            part = dot(rows, w[k : k + 3].reshape(192, 512), NT)
            ah[side, 2 - a : 8] += part.reshape(n, 2, 16, 192)
    edge_send(0, lambda side, t: summed_columns(ah[side, t].reshape(32, 192)).reshape(2, 16, 64))

    for a in range(3):
        n = 6 + a
        for b in range(3):
            k = 9 * a + 3 * b
            lo = 16 if b == 2 else 0
            to = 16 if b == 0 else 0
            size = 64 if b == 1 else 48
            rows = xg[0:n, :, lo : lo + size].reshape(n * 2 * size, 512)
            part = dot(rows, w[k : k + 3].reshape(192, 512), NT)
            acc[2 - a : 8, :, to : to + size, :] += part.reshape(n, 2, size, 192)

    def columns(t, _):
        pre[t, :, 16:80] = summed_columns(acc[t].reshape(128, 192)).reshape(2, 64, 64)
        return 0

    lax.fori_loop(0, 8, columns, 0)

    edge_wait(0)
    for t in range(8):
        pre[t, :, 16:32] += edge_rows(0, 1, t)
        pre[t, :, 64:80] += edge_rows(0, 0, t)
        v = pre[t, :, 16:80]
        s = 1.0 / (1.0 + jnp.exp(-v))
        act[t] = v * s
        pre[t, :, 16:80] = s * (1.0 + v * (1.0 - s))
    edge_send(2, lambda side, t: act[t, :, 48 * side : 48 * side + 16])

    def stacked(rows, t):
        v = rows(t)
        zero = jnp.zeros_like(v)
        return jnp.concatenate([rows(t - 2) if t > 1 else zero, rows(t - 1) if t > 0 else zero, v], axis=-1)

    for t in range(8):
        act3[t] = stacked(lambda u: act[u], t).astype(BF)
    act3t[...] = dot(eye_in[...], act3[...].reshape(1024, 192), NT).astype(BF)

    edge_wait(1)
    for t in range(8):
        ga[t, :, 0:16] += edge_rows(1, 1, t)
        ga[t, :, 48:64] += edge_rows(1, 0, t)
        pre[t, :, 16:80] = ga[t] * pre[t, :, 16:80]
    edge_send(3, lambda side, t: pre[t, :, 16 + 48 * side : 32 + 48 * side])

    edge_wait(2)
    for t in range(8):
        for side in range(2):
            qh[side, t, :, :, 0:64] = edge_rows(2, 1 - side, t)
    for side in range(2):
        stack = jnp.concatenate(
            [stacked(lambda u: qh[side, u, :, :, 0:64], t).reshape(32, 192) for t in range(8)], axis=0
        ).astype(BF)
        hal3t[side] = dot(eye_in[...], stack, NT).astype(BF)

    for b in range(3):
        part = dot(act3t[...], g[:, :, :, 768 * b : 768 * b + 768].reshape(1024, 768), NN)
        if b != 1:
            part = part + dot(hal3t[b // 2], gh[b // 2].reshape(256, 768), NN)
        for e in range(3):
            k = 3 * b + e
            gws[3 * k : 3 * k + 3] = part[:, 256 * e : 256 * e + 256].astype(BF).reshape(3, 64, 256)
    gws[27] = jnp.zeros((64, 256), BF)

    size, place = (4, 3), (0, 4)

    def x_copy(d, i):
        to = (x + d) % 4
        return remote(
            gws.at[pl.ds(7 * to + place[i], size[i])], ra.at[d - 1, place[i] : place[i] + size[i]],
            a_s.at[d - 1, i], a_r.at[d - 1, i], dev(to, y, z, c),
        )

    for i in range(2):
        for d in (2, 1, 3):
            x_copy(d, i).start()

    edge_wait(3)
    for t in range(8):
        pre[t, :, 0:16] = edge_rows(3, 1, t)
        pre[t, :, 80:96] = edge_rows(3, 0, t)

    col96 = lax.broadcasted_iota(jnp.int32, (192, 64), 0) % 16

    def shifted(t, _):
        part = pre[t].reshape(192, 64)
        after = jnp.where(col96 == 15, 0.0, pltpu.roll(part, 191, 0))
        before = jnp.where(col96 == 0, 0.0, pltpu.roll(part, 1, 0))
        gp3[t] = jnp.concatenate([after, part, before], axis=-1).reshape(2, 96, 192).astype(BF)
        return 0

    lax.fori_loop(0, 8, shifted, 0)
    gi[...] = jnp.zeros_like(gi)
    for a in range(3):
        n = 6 + a
        for b in range(3):
            k = 9 * a + 3 * b
            rows = gp3[2 - a : 8, :, 16 * (2 - b) : 16 * (2 - b) + 64, :].reshape(n * 128, 192)
            part = dot(rows, w[k : k + 3].reshape(192, 512), NN)
            gi[0:n] += part.reshape(n, 2, 64, 512)

    for half in range(2):
        for f in range(2):
            pb[half, f] = gi[4 * half + 2 * (1 - c) + f].astype(BF)
    pair_copy = remote(pb, rp, pr_s, pr_r, dev(x, y, z, 1 - c))
    pair_copy.start()

    sbf[:, 56:64] = jnp.zeros((8, 8, 256), F32)

    def z_copy(d, i):
        to = (z + d) % NZ
        half = slice(32 * i, 32 * i + 32)
        return remote(sb.at[to, half], rb.at[d - 1, half], b_s.at[d - 1, i], b_r.at[d - 1, i], dev(x, y, to, c))

    def x_sum(i):
        for d in range(1, 4):
            x_copy(d, i).wait_recv()
        for j in range(place[i], place[i] + size[i]):
            total = gws[7 * x + j].astype(F32)
            for d in range(3):
                total = total + ra[d, j].astype(F32)
            sbf[:, 8 * j : 8 * j + 8] = total.reshape(8, 8, 256)
        sb[:, 32 * i : 32 * i + 32] = sbf[:, 32 * i : 32 * i + 32].astype(BF)
        for d in (4, 3, 5, 2, 6, 1, 7):
            z_copy(d, i).start()

    def z_sum(i):
        half = slice(32 * i, 32 * i + 32)
        for d in range(1, NZ):
            z_copy(d, i).wait_recv()
        total = sb[z, half].astype(F32)
        for d in range(NZ - 1):
            total = total + rb[d, half].astype(F32)
        fc[half] = (total * scale).astype(BF)

    x_sum(0)
    pair_copy.wait_recv()
    for half in range(2):
        for f in range(2):
            ps[half, f] = (gi[4 * half + 2 * c + f] + rp[half, f].astype(F32)).astype(BF)

    def y_copy(d):
        to = (y + d) % 4
        return remote(ps.at[to % 2, :, to // 2], rr.at[d - 1], rs_s.at[d - 1], rs_r.at[d - 1], dev(x, to, z, c))

    for d in (2, 1, 3):
        y_copy(d).start()

    x_sum(1)
    z_sum(0)
    z_sum(1)

    def out_copy(to_x):
        return remote(fc, rc.at[x], c_s.at[to_x], c_r.at[x], dev(to_x, y_out, z, c))

    for to_x in range(4):
        mine = jnp.logical_and(x == to_x, y == y_out)

        @pl.when(mine)
        def _():
            pltpu.make_async_copy(fc, rc.at[x], c_r.at[x]).start()

        @pl.when(jnp.logical_not(mine))
        def _():
            out_copy(to_x).start()

    for d in range(1, 4):
        y_copy(d).wait_recv()
    total = ps[ylo, :, yhi].astype(F32)
    for d in range(3):
        total = total + rr[d].astype(F32)
    gi_out[...] = total.astype(BF)

    for part in range(4):
        pltpu.make_async_copy(fc, rc.at[part], c_r.at[part]).wait()
        v = rc[part].astype(F32)
        for j in range(7):
            k, a = (7 * part + j) // 3, (7 * part + j) % 3
            if k < 9:
                gw_out[9 * a + k] = v[8 * j : 8 * j + 8]

    def sent(copy):
        copy.wait_send()

    for n in range(2):
        for i in range(10):
            gather(n, i).wait_send()
    for part in range(4):
        for slot in range(2):
            z_sends(part, slot, sent)
    for slot in range(2):
        @pl.when(pos != slot)
        def _():
            for i in range(4):
                along_x(slot, i).wait_send()

    for n in range(4):
        for side in range(2):
            edge_copy(n, side).wait_send()
    pair_copy.wait_send()
    for d in range(1, 4):
        x_copy(d, 0).wait_send()
        x_copy(d, 1).wait_send()
        y_copy(d).wait_send()
    for d in range(1, NZ):
        z_copy(d, 0).wait_send()
        z_copy(d, 1).wait_send()
    for to_x in range(4):
        @pl.when(jnp.logical_not(jnp.logical_and(x == to_x, y == y_out)))
        def _():
            out_copy(to_x).wait_send()


def on_device(latent, out_grad, w_first, w_second):
    wt = jnp.swapaxes(w_first, 1, 2)
    scale = 1.0 / math.sqrt(131072.0)
    hbm = pl.BlockSpec(memory_space=pl.ANY)
    vmem = pl.BlockSpec(memory_space=pltpu.VMEM)
    dma = pltpu.SemaphoreType.DMA
    grad_input, grad_w2 = pl.pallas_call(
        functools.partial(body, scale),
        out_shape=(
            jax.ShapeDtypeStruct((2, 64, 512), BF),
            jax.ShapeDtypeStruct((27, 8, 256), F32),
        ),
        in_specs=[hbm, hbm, hbm, hbm, vmem, vmem],
        out_specs=(vmem, vmem),
        scratch_shapes=[
            pltpu.VMEM((8, 2, 64, 512), BF),
            pltpu.VMEM((8, 2, 256, 256), BF),
            pltpu.VMEM((27, 2, 32, 512), BF),
            pltpu.VMEM((192, 2304), BF),
            pltpu.VMEM((8, 2, 64, 2304), BF),
            pltpu.VMEM((2, 8, 2, 16, 768), BF),
            pltpu.VMEM((8, 2, 64, 192), F32),
            pltpu.VMEM((2, 8, 2, 16, 192), F32),
            pltpu.VMEM((8, 2, 64, 192), F32),
            pltpu.VMEM((2, 8, 2, 16, 192), F32),
            pltpu.VMEM((8, 2, 96, 64), F32),
            pltpu.VMEM((8, 2, 64, 64), F32),
            pltpu.VMEM((4, 2, 4, 2, 16, 128), BF),
            pltpu.VMEM((4, 2, 4, 2, 16, 128), BF),
            pltpu.VMEM((8, 2, 64, 64), F32),
            pltpu.VMEM((8, 2, 96, 192), BF),
            pltpu.VMEM((8, 2, 64, 192), BF),
            pltpu.VMEM((192, 1024), BF),
            pltpu.VMEM((2, 192, 256), BF),
            pltpu.VMEM((8, 2, 64, 512), F32),
            pltpu.VMEM((2, 2, 2, 64, 512), BF),
            pltpu.VMEM((2, 2, 2, 64, 512), BF),
            pltpu.VMEM((2, 2, 2, 64, 512), BF),
            pltpu.VMEM((3, 2, 64, 512), BF),
            pltpu.VMEM((28, 64, 256), BF),
            pltpu.VMEM((3, 7, 64, 256), BF),
            pltpu.VMEM((8, 64, 256), F32),
            pltpu.VMEM((8, 64, 256), BF),
            pltpu.VMEM((7, 64, 256), BF),
            pltpu.VMEM((64, 256), BF),
            pltpu.VMEM((4, 64, 256), BF),
            dma((3,)), dma((3, 9)),
            dma((2, 10)), dma((2, 10)),
            dma((4, 2, 2)), dma((4, 2)),
            dma((2, 4)), dma((2, 4)),
            dma((4, 2)), dma((4, 2)),
            dma, dma,
            dma((3,)), dma((3,)),
            dma((3, 2)), dma((3, 2)),
            dma((7, 2)), dma((7, 2)),
            dma((4,)), dma((4,)),
        ],
        compiler_params=pltpu.CompilerParams(
            collective_id=0, has_side_effects=True, vmem_limit_bytes=56 * 1024 * 1024
        ),
    )(
        latent.reshape(2, 64, 512),
        out_grad.reshape(2, 256, 256),
        wt,
        w_second,
        jnp.asarray(cell_sums(), BF),
        jnp.asarray(np.eye(192, dtype=np.float32), BF),
    )
    return grad_input.reshape(1, 2, 4, 16, 512), jnp.swapaxes(grad_w2, 0, 1)


def solution(mesh):
    placed = (
        P("dp", "tm", "height", None, None),
        P("dp", "tm", "height", None, None),
        P(None, None, "height"),
        P(),
    )
    return jax.shard_map(
        on_device,
        mesh=mesh,
        in_specs=placed,
        out_specs=(P("dp", "tm", "height", None, None), P(("tm", "height"), None, None)),
        check_vma=False,
    )
```

```python
import functools
import math

import jax
import jax.numpy as jnp
import numpy as np
from jax import lax
from jax.experimental import pallas as pl
from jax.experimental.pallas import tpu as pltpu
from jax.sharding import PartitionSpec as P

MESH = pl.DeviceIdType.MESH
BF = jnp.bfloat16
F32 = jnp.float32
NZ = 8
NT = (((1,), (1,)), ((), ()))
NN = (((1,), (0,)), ((), ()))


def cell_sums():
    main = np.zeros((3, 3, 4, 16, 8, 32), np.float32)
    edge = np.zeros((2, 3, 16, 8, 32), np.float32)
    for b in range(3):
        for e in range(3):
            for c in range(16):
                cols = [2 * c + q + 1 - e for q in range(2) if 0 <= 2 * c + q + 1 - e < 32]
                for h in range(4):
                    for p in range(2):
                        row = 2 * h + p + 1 - b
                        if 0 <= row < 8:
                            main[b, e, h, c, row, cols] = 1.0
                if b == 0:
                    edge[0, e, c, 0, cols] = 1.0
                if b == 2:
                    edge[1, e, c, 7, cols] = 1.0
    return np.concatenate([main.reshape(576, 256), edge.reshape(96, 256)], axis=0)


def tap_places():
    middle = [(1, e, a) for e in range(3) for a in range(3)]
    rest = [middle[8]] + [(b, e, a) for b in (0, 2) for e in range(3) for a in range(3)]
    places = []
    for x in range(4):
        places += middle[2 * x : 2 * x + 2] + rest[5 * x : 5 * x + 5]
    return places


def dot(a, b, dims):
    return lax.dot_general(a, b, dims, preferred_element_type=F32)


def body(
    scale,
    lat_in, og_in, wt_in, w2_in, sums_in, eye_in,
    gi_out, gw_out,
    xg, og, w, w2, g, gh, acc, ah, q, qh, pre, ga, es, er,
    act, gp3, act3, act3t, gi, pb, rp, ps, rr, gws, ra, sbf, sb, rb, fc, rc,
    loc_s, w2_s, ag_s, ag_r, wz_s, wz_r, wx_s, wx_r, e_s, e_r, pr_s, pr_r, rs_s, rs_r,
    a_s, a_r, b_s, b_r, c_s, c_r,
):
    x = lax.axis_index("dp")
    tm = lax.axis_index("tm")
    height = lax.axis_index("height")
    c = tm % 2
    ylo = tm // 2
    z = height % NZ
    yhi = height // NZ
    y = 2 * yhi + ylo
    y_out = 2 * ylo + yhi

    def dev(x_, y_, z_, c_):
        return (x_, (y_ % 2) * 2 + c_, (y_ // 2) * NZ + z_)

    up_y, down_y = (y + 1) % 4, (y + 3) % 4
    up_z, down_z = (z + 1) % NZ, (z + NZ - 1) % NZ
    up_x, down_x = (x + 1) % 4, (x + 3) % 4
    far_y, far_x = (y + 2) % 4, (x + 2) % 4

    def remote(src, dst, ssem, rsem, target):
        return pltpu.make_async_remote_copy(
            src_ref=src, dst_ref=dst, send_sem=ssem, recv_sem=rsem,
            device_id=target, device_id_type=MESH,
        )

    def slab(ref, y_, c_, f):
        return ref.at[2 * (2 * (y_ % 2) + c_) + f, y_ // 2]

    def block(ref, y_, c_):
        return ref.at[pl.ds(2 * (2 * (y_ % 2) + c_), 2), y_ // 2]

    pos = (z + NZ - (4 * c + 2 * ylo)) % NZ
    source = pos < 2
    base = 64 * (4 * yhi + 2 * c + ylo)
    own = [
        pltpu.make_async_copy(lat_in, block(xg, y, c), loc_s.at[0]),
        pltpu.make_async_copy(og_in, block(og, y, c), loc_s.at[1]),
    ]
    own_w = pltpu.make_async_copy(wt_in, w.at[:, pos % 2], loc_s.at[2])
    w2_copies = [
        pltpu.make_async_copy(
            w2_in.at[9 * a + k, pl.ds(pl.multiple_of(base, 64), 64)],
            w2.at[64 * a : 64 * a + 64, 256 * k : 256 * k + 256],
            w2_s.at[a, k],
        )
        for a in range(3)
        for k in range(9)
    ]

    @pl.when(source)
    def _():
        own_w.start()

    for copy in own:
        copy.start()

    barrier = pltpu.get_barrier_semaphore()

    def greet(target):
        pl.semaphore_signal(barrier, inc=1, device_id=target, device_id_type=MESH)

    greet(dev(x, y, z, 1 - c))
    for d in (1, 3, 2):
        greet(dev(x, (y + d) % 4, z, c))
        greet(dev((x + d) % 4, y, z, c))
    for d in (1, 7, 2, 6, 3, 5, 4):
        greet(dev(x, y, (z + d) % NZ, c))
    swaps = y != y_out

    @pl.when(swaps)
    def _():
        for d in range(1, 4):
            greet(dev((x + d) % 4, y_out, z, c))

    for copy in w2_copies:
        copy.start()
    acc[...] = jnp.zeros_like(acc)
    ah[...] = jnp.zeros_like(ah)

    @pl.when(source)
    def _():
        own_w.wait()

    for copy in own:
        copy.wait()
    pl.semaphore_wait(barrier, 14 + 3 * swaps.astype(jnp.int32))

    arrays = (og, xg)

    def gather(n, i):
        ref = arrays[n]
        up, down, mate = dev(x, up_y, z, c), dev(x, down_y, z, c), dev(x, y, z, 1 - c)
        place, target = {
            0: lambda: (slab(ref, y, c, 0), up),
            1: lambda: (slab(ref, y, c, 1), down),
            2: lambda: (slab(ref, y, c, 1), up),
            3: lambda: (slab(ref, y, c, 0), down),
            4: lambda: (block(ref, y, c), mate),
            5: lambda: (slab(ref, down_y, c, 0), up),
            6: lambda: (slab(ref, up_y, c, 1), down),
            7: lambda: (block(ref, down_y, c), mate),
            8: lambda: (block(ref, up_y, c), mate),
            9: lambda: (block(ref, far_y, c), mate),
        }[i]()
        return remote(place, place, ag_s.at[n, i], ag_r.at[n, i], target)

    reach = (4, 4, 3, 3, 3)
    cuts = (16, 20, 24, 27)

    def share(part, slot):
        if part < 2:
            return w.at[pl.ds(4 * x + 2 * part, 2), slot]
        return w.at[cuts[part - 2] : cuts[part - 1], slot]

    def along_z(part, slot, way):
        target = dev(x, y, up_z if way == 0 else down_z, c)
        place = share(part, slot)
        return remote(place, place, wz_s.at[part, slot, way], wz_r.at[part, slot], target)

    def z_sends(part, slot, act_on):
        far = (pos + NZ - slot) % NZ
        r = reach[part]

        @pl.when(far < r)
        def _():
            act_on(along_z(part, slot, 0))

        @pl.when(jnp.logical_or(far == 0, far > r + 1))
        def _():
            act_on(along_z(part, slot, 1))

    def goes_on(part, slot):
        far = (pos + NZ - slot) % NZ
        r = reach[part]
        return jnp.logical_and(far != 0, jnp.logical_or(far < r, far > r + 1))

    def along_x(slot, i):
        up, down = dev(up_x, y, z, c), dev(down_x, y, z, c)
        first, target = (
            (4 * x, up), (4 * x + 2, up), (4 * x + 2, down), (4 * x, down),
            (4 * down_x, up), (4 * up_x + 2, down),
        )[i]
        place = w.at[pl.ds(first, 2), slot]
        return remote(place, place, wx_s.at[slot, i], wx_r.at[slot, i], target)

    def start(copy):
        copy.start()

    closer = jnp.where(jnp.logical_and(pos >= 1, pos <= 4), 1, 0)
    slots = (closer, 1 - closer)
    own_slot = pos % 2

    @pl.when(source)
    def _():
        z_sends(0, own_slot, start)
        z_sends(1, own_slot, start)

    for i in range(5):
        gather(0, i).start()

    @pl.when(source)
    def _():
        z_sends(2, own_slot, start)
        z_sends(3, own_slot, start)
        z_sends(4, own_slot, start)

    for i in range(5):
        gather(1, i).start()

    def pass_on(part, slot):
        @pl.when(pos != slot if part < 2 else goes_on(part, slot))
        def _():
            along_z(part, slot, 0).wait_recv()
            z_sends(part, slot, start)
            if part < 2:
                along_x(slot, part).start()
                along_x(slot, 3 - part).start()

    def pass_end(part, slot):
        @pl.when(jnp.logical_and(pos != slot, jnp.logical_not(goes_on(part, slot))))
        def _():
            along_z(part, slot, 0).wait_recv()

    def pass_x(slot):
        @pl.when(pos != slot)
        def _():
            along_x(slot, 0).wait_recv()
            along_x(slot, 4).start()
            along_x(slot, 2).wait_recv()
            along_x(slot, 5).start()

    def pass_y(n):
        gather(n, 0).wait_recv()
        gather(n, 5).start()
        gather(n, 1).wait_recv()
        gather(n, 6).start()

    def pass_mate(n):
        gather(n, 2).wait_recv()
        gather(n, 7).start()
        gather(n, 3).wait_recv()
        gather(n, 8).start()

    def pass_far(n):
        gather(n, 5).wait_recv()
        gather(n, 6).wait_recv()
        gather(n, 9).start()

    near, far = slots
    close = jnp.logical_or(pos < 3, pos == 7)

    def pass_z(*steps):
        for part, slot in steps:
            pass_on(part, slot)

    @pl.when(close)
    def _():
        pass_z((0, near), (1, near))
        pass_y(0)
        pass_z((0, far), (1, far), (2, near))
        pass_mate(0)
        pass_x(near)
        pass_z((2, far), (3, near))
        pass_y(1)
        pass_far(0)
        pass_x(far)
        pass_z((3, far), (4, near))
        pass_mate(1)
        pass_z((4, far))
        pass_far(1)

    @pl.when(jnp.logical_not(close))
    def _():
        pass_y(0)
        pass_z((0, near), (1, near))
        pass_mate(0)
        pass_z((0, far), (1, far))
        pass_y(1)
        pass_far(0)
        pass_z((2, near))
        pass_x(near)
        pass_mate(1)
        pass_z((2, far), (3, near))
        pass_far(1)

    for i in (4, 7, 8, 9):
        gather(0, i).wait_recv()

    def sums_of(f, band):
        part = dot(sums_in[...], og[f, band], NN)
        for k in range(9):
            g[f, band, :, 256 * k : 256 * k + 256] = part[64 * k : 64 * k + 64].astype(BF)
        for k in range(6):
            lane = 256 * (k % 3)
            gh[k // 3, f, band, :, lane : lane + 256] = part[576 + 16 * k : 592 + 16 * k].astype(BF)

    def sum_step(f, _):
        sums_of(f, 0)
        sums_of(f, 1)
        return 0

    lax.fori_loop(0, 4, sum_step, 0)

    @pl.when(jnp.logical_not(close))
    def _():
        pass_x(far)
        pass_z((3, far), (4, near), (4, far))

    lax.fori_loop(4, 8, sum_step, 0)
    for copy in w2_copies:
        copy.wait()

    def edge_copy(n, side):
        target = dev(x, y, down_z if side == 0 else up_z, c)
        return remote(es.at[n, side], er.at[n, side], e_s.at[n, side], e_r.at[n, side], target)

    def edge_send(n, rows):
        for side in range(2):
            for t in range(4):
                es[n, side, t] = jnp.concatenate([rows(side, t), rows(side, t + 4)], axis=-1).astype(BF)
            edge_copy(n, side).start()

    def edge_wait(n):
        for side in range(2):
            edge_copy(n, side).wait_recv()

    last, first = z == NZ - 1, z == 0

    def edge_rows(n, side, t):
        v = er[n, side, t % 4][:, :, 64 * (t // 4) : 64 * (t // 4) + 64].astype(F32)
        if side == 0:
            return jnp.where(last, jnp.stack([v[1], jnp.zeros_like(v[1])]), v)
        return jnp.where(first, jnp.stack([jnp.zeros_like(v[0]), v[0]]), v)

    def through_time(ref, t):
        out = ref[t, :, :, 128:192]
        if t < 7:
            out = out + ref[t + 1, :, :, 64:128]
        if t < 6:
            out = out + ref[t + 2, :, :, 0:64]
        return out

    for side in range(2):
        lanes = slice(1536 * side, 1536 * side + 768)
        qh[side] = dot(gh[side].reshape(256, 768), w2[:, lanes], NT).reshape(8, 2, 16, 192)
    edge_send(1, lambda side, t: through_time(qh.at[side], t))
    q[...] = dot(g[...].reshape(1024, 2304), w2[...], NT).reshape(8, 2, 64, 192)
    for t in range(8):
        ga[t] = through_time(q, t)

    for i in (4, 7, 8, 9):
        gather(1, i).wait_recv()
    for slot in range(2):
        for part in range(2, 5):
            pass_end(part, slot)

        @pl.when(pos != slot)
        def _():
            for i in (1, 3, 4, 5):
                along_x(slot, i).wait_recv()

    def summed_columns(part):
        rows = part.shape[0]
        col = lax.broadcasted_iota(jnp.int32, (rows, 64), 0) % 16
        before = jnp.where(col == 0, 0.0, pltpu.roll(part[:, 0:64], 1, 0))
        after = jnp.where(col == 15, 0.0, pltpu.roll(part[:, 128:192], rows - 1, 0))
        return before + part[:, 64:128] + after

    for side in range(2):
        for a in range(3):
            n = 6 + a
            k = 9 * a + 6 * (1 - side)
            rows = xg[0:n, :, 48 * side : 48 * side + 16].reshape(n * 32, 512)
            part = dot(rows, w[k : k + 3].reshape(192, 512), NT)
            ah[side, 2 - a : 8] += part.reshape(n, 2, 16, 192)
    edge_send(0, lambda side, t: summed_columns(ah[side, t].reshape(32, 192)).reshape(2, 16, 64))

    for a in range(3):
        n = 6 + a
        for b in range(3):
            k = 9 * a + 3 * b
            lo = 16 if b == 2 else 0
            to = 16 if b == 0 else 0
            size = 64 if b == 1 else 48
            rows = xg[0:n, :, lo : lo + size].reshape(n * 2 * size, 512)
            part = dot(rows, w[k : k + 3].reshape(192, 512), NT)
            acc[2 - a : 8, :, to : to + size, :] += part.reshape(n, 2, size, 192)

    def columns(t, _):
        pre[t, :, 16:80] = summed_columns(acc[t].reshape(128, 192)).reshape(2, 64, 64)
        return 0

    lax.fori_loop(0, 8, columns, 0)

    edge_wait(0)
    for t in range(8):
        pre[t, :, 16:32] += edge_rows(0, 1, t)
        pre[t, :, 64:80] += edge_rows(0, 0, t)
        v = pre[t, :, 16:80]
        s = 1.0 / (1.0 + jnp.exp(-v))
        act[t] = v * s
        pre[t, :, 16:80] = s * (1.0 + v * (1.0 - s))
    edge_send(2, lambda side, t: act[t, :, 48 * side : 48 * side + 16])

    def stacked(rows, t):
        v = rows(t)
        zero = jnp.zeros_like(v)
        return jnp.concatenate([rows(t - 2) if t > 1 else zero, rows(t - 1) if t > 0 else zero, v], axis=-1)

    for t in range(8):
        act3[t] = stacked(lambda u: act[u], t).astype(BF)
    act3t[...] = dot(eye_in[...], act3[...].reshape(1024, 192), NT).astype(BF)

    first_place, size = (0, 2, 6), (2, 4, 1)
    places = tap_places()

    def x_copy(d, i):
        to = (x + d) % 4
        lo = first_place[i]
        return remote(
            gws.at[pl.ds(7 * to + lo, size[i])], ra.at[d - 1, lo : lo + size[i]],
            a_s.at[d - 1, i], a_r.at[d - 1, i], dev(to, y, z, c),
        )

    def keep(b, part):
        for e in range(3):
            for a in range(3):
                gws[places.index((b, e, a))] = part[64 * a : 64 * a + 64, 256 * e : 256 * e + 256].astype(BF)

    def own_cells(b):
        return dot(act3t[...], g[:, :, :, 768 * b : 768 * b + 768].reshape(1024, 768), NN)

    keep(1, own_cells(1))
    for d in (2, 1, 3):
        x_copy(d, 0).start()

    edge_wait(1)
    for t in range(8):
        ga[t, :, 0:16] += edge_rows(1, 1, t)
        ga[t, :, 48:64] += edge_rows(1, 0, t)
        pre[t, :, 16:80] = ga[t] * pre[t, :, 16:80]
    edge_send(3, lambda side, t: pre[t, :, 16 + 48 * side : 32 + 48 * side])

    parts = (own_cells(0), own_cells(2))
    edge_wait(2)
    for t in range(8):
        for side in range(2):
            qh[side, t, :, :, 0:64] = edge_rows(2, 1 - side, t)
    for side in range(2):
        stack = jnp.concatenate(
            [stacked(lambda u: qh[side, u, :, :, 0:64], t).reshape(32, 192) for t in range(8)], axis=0
        ).astype(BF)
        hal3t = dot(eye_in[...], stack, NT).astype(BF)
        keep(2 * side, parts[side] + dot(hal3t, gh[side].reshape(256, 768), NN))
    gws[27] = jnp.zeros((64, 256), BF)
    for i in (1, 2):
        for d in (2, 1, 3):
            x_copy(d, i).start()

    edge_wait(3)
    for t in range(8):
        pre[t, :, 0:16] = edge_rows(3, 1, t)
        pre[t, :, 80:96] = edge_rows(3, 0, t)

    col96 = lax.broadcasted_iota(jnp.int32, (192, 64), 0) % 16

    def shifted(t, _):
        part = pre[t].reshape(192, 64)
        after = jnp.where(col96 == 15, 0.0, pltpu.roll(part, 191, 0))
        before = jnp.where(col96 == 0, 0.0, pltpu.roll(part, 1, 0))
        gp3[t] = jnp.concatenate([after, part, before], axis=-1).reshape(2, 96, 192).astype(BF)
        return 0

    lax.fori_loop(0, 8, shifted, 0)
    gi[...] = jnp.zeros_like(gi)
    for a in range(3):
        n = 6 + a
        for b in range(3):
            k = 9 * a + 3 * b
            rows = gp3[2 - a : 8, :, 16 * (2 - b) : 16 * (2 - b) + 64, :].reshape(n * 128, 192)
            part = dot(rows, w[k : k + 3].reshape(192, 512), NN)
            gi[0:n] += part.reshape(n, 2, 64, 512)

    for half in range(2):
        for f in range(2):
            pb[half, f] = gi[4 * half + 2 * (1 - c) + f].astype(BF)
    pair_copy = remote(pb, rp, pr_s, pr_r, dev(x, y, z, 1 - c))
    pair_copy.start()

    sbf[:, 56:64] = jnp.zeros((8, 8, 256), F32)

    def rows_of(i):
        return slice(8 * first_place[i], 8 * first_place[i] + max(8 * size[i], 16))

    def z_copy(d, i):
        to = (z + d) % NZ
        part = rows_of(i)
        return remote(sb.at[to, part], rb.at[d - 1, part], b_s.at[d - 1, i], b_r.at[d - 1, i], dev(x, y, to, c))

    def x_sum(i):
        for d in range(1, 4):
            x_copy(d, i).wait_recv()
        for j in range(first_place[i], first_place[i] + size[i]):
            total = gws[7 * x + j].astype(F32)
            for d in range(3):
                total = total + ra[d, j].astype(F32)
            sbf[:, 8 * j : 8 * j + 8] = total.reshape(8, 8, 256)
        part = rows_of(i)
        sb[:, part] = sbf[:, part].astype(BF)
        for d in (4, 3, 5, 2, 6, 1, 7):
            z_copy(d, i).start()

    def z_sum(i):
        part = rows_of(i)
        for d in range(1, NZ):
            z_copy(d, i).wait_recv()
        total = sb[z, part].astype(F32)
        for d in range(NZ - 1):
            total = total + rb[d, part].astype(F32)
        fc[part] = (total * scale).astype(BF)

    x_sum(0)
    pair_copy.wait_recv()
    for half in range(2):
        for f in range(2):
            ps[half, f] = (gi[4 * half + 2 * c + f] + rp[half, f].astype(F32)).astype(BF)

    def y_copy(d):
        to = (y + d) % 4
        return remote(ps.at[to % 2, :, to // 2], rr.at[d - 1], rs_s.at[d - 1], rs_r.at[d - 1], dev(x, to, z, c))

    for d in (2, 1, 3):
        y_copy(d).start()

    x_sum(1)
    z_sum(0)
    x_sum(2)
    z_sum(1)
    z_sum(2)

    def out_copy(to_x):
        return remote(fc, rc.at[x], c_s.at[to_x], c_r.at[x], dev(to_x, y_out, z, c))

    for to_x in range(4):
        mine = jnp.logical_and(x == to_x, y == y_out)

        @pl.when(mine)
        def _():
            pltpu.make_async_copy(fc, rc.at[x], c_r.at[x]).start()

        @pl.when(jnp.logical_not(mine))
        def _():
            out_copy(to_x).start()

    for d in range(1, 4):
        y_copy(d).wait_recv()
    total = ps[ylo, :, yhi].astype(F32)
    for d in range(3):
        total = total + rr[d].astype(F32)
    gi_out[...] = total.astype(BF)

    for part in range(4):
        pltpu.make_async_copy(fc, rc.at[part], c_r.at[part]).wait()
        v = rc[part].astype(F32)
        for j in range(7):
            if 7 * part + j < 27:
                b, e, a = places[7 * part + j]
                gw_out[9 * a + 3 * b + e] = v[8 * j : 8 * j + 8]

    def sent(copy):
        copy.wait_send()

    for n in range(2):
        for i in range(10):
            gather(n, i).wait_send()
    for part in range(5):
        for slot in range(2):
            z_sends(part, slot, sent)
    for slot in range(2):
        @pl.when(pos != slot)
        def _():
            for i in range(6):
                along_x(slot, i).wait_send()

    for n in range(4):
        for side in range(2):
            edge_copy(n, side).wait_send()
    pair_copy.wait_send()
    for d in range(1, 4):
        for i in range(3):
            x_copy(d, i).wait_send()
        y_copy(d).wait_send()
    for d in range(1, NZ):
        for i in range(3):
            z_copy(d, i).wait_send()
    for to_x in range(4):
        @pl.when(jnp.logical_not(jnp.logical_and(x == to_x, y == y_out)))
        def _():
            out_copy(to_x).wait_send()


def on_device(latent, out_grad, w_first, w_second):
    wt = jnp.swapaxes(w_first, 1, 2)
    scale = 1.0 / math.sqrt(131072.0)
    hbm = pl.BlockSpec(memory_space=pl.ANY)
    vmem = pl.BlockSpec(memory_space=pltpu.VMEM)
    dma = pltpu.SemaphoreType.DMA
    grad_input, grad_w2 = pl.pallas_call(
        functools.partial(body, scale),
        out_shape=(
            jax.ShapeDtypeStruct((2, 64, 512), BF),
            jax.ShapeDtypeStruct((27, 8, 256), F32),
        ),
        in_specs=[hbm, hbm, hbm, hbm, vmem, vmem],
        out_specs=(vmem, vmem),
        scratch_shapes=[
            pltpu.VMEM((8, 2, 64, 512), BF),
            pltpu.VMEM((8, 2, 256, 256), BF),
            pltpu.VMEM((27, 2, 32, 512), BF),
            pltpu.VMEM((192, 2304), BF),
            pltpu.VMEM((8, 2, 64, 2304), BF),
            pltpu.VMEM((2, 8, 2, 16, 768), BF),
            pltpu.VMEM((8, 2, 64, 192), F32),
            pltpu.VMEM((2, 8, 2, 16, 192), F32),
            pltpu.VMEM((8, 2, 64, 192), F32),
            pltpu.VMEM((2, 8, 2, 16, 192), F32),
            pltpu.VMEM((8, 2, 96, 64), F32),
            pltpu.VMEM((8, 2, 64, 64), F32),
            pltpu.VMEM((4, 2, 4, 2, 16, 128), BF),
            pltpu.VMEM((4, 2, 4, 2, 16, 128), BF),
            pltpu.VMEM((8, 2, 64, 64), F32),
            pltpu.VMEM((8, 2, 96, 192), BF),
            pltpu.VMEM((8, 2, 64, 192), BF),
            pltpu.VMEM((192, 1024), BF),
            pltpu.VMEM((8, 2, 64, 512), F32),
            pltpu.VMEM((2, 2, 2, 64, 512), BF),
            pltpu.VMEM((2, 2, 2, 64, 512), BF),
            pltpu.VMEM((2, 2, 2, 64, 512), BF),
            pltpu.VMEM((3, 2, 64, 512), BF),
            pltpu.VMEM((28, 64, 256), BF),
            pltpu.VMEM((3, 7, 64, 256), BF),
            pltpu.VMEM((8, 64, 256), F32),
            pltpu.VMEM((8, 64, 256), BF),
            pltpu.VMEM((7, 64, 256), BF),
            pltpu.VMEM((64, 256), BF),
            pltpu.VMEM((4, 64, 256), BF),
            dma((3,)), dma((3, 9)),
            dma((2, 10)), dma((2, 10)),
            dma((5, 2, 2)), dma((5, 2)),
            dma((2, 6)), dma((2, 6)),
            dma((4, 2)), dma((4, 2)),
            dma, dma,
            dma((3,)), dma((3,)),
            dma((3, 3)), dma((3, 3)),
            dma((7, 3)), dma((7, 3)),
            dma((4,)), dma((4,)),
        ],
        compiler_params=pltpu.CompilerParams(
            collective_id=0, has_side_effects=True, vmem_limit_bytes=56 * 1024 * 1024
        ),
    )(
        latent.reshape(2, 64, 512),
        out_grad.reshape(2, 256, 256),
        wt,
        w_second,
        jnp.asarray(cell_sums(), BF),
        jnp.asarray(np.eye(192, dtype=np.float32), BF),
    )
    return grad_input.reshape(1, 2, 4, 16, 512), jnp.swapaxes(grad_w2, 0, 1)


def solution(mesh):
    placed = (
        P("dp", "tm", "height", None, None),
        P("dp", "tm", "height", None, None),
        P(None, None, "height"),
        P(),
    )
    return jax.shard_map(
        on_device,
        mesh=mesh,
        in_specs=placed,
        out_specs=(P("dp", "tm", "height", None, None), P(("tm", "height"), None, None)),
        check_vma=False,
    )
```

```python
import functools
import math

import jax
import jax.numpy as jnp
import numpy as np
from jax import lax
from jax.experimental import pallas as pl
from jax.experimental.pallas import tpu as pltpu
from jax.sharding import PartitionSpec as P

MESH = pl.DeviceIdType.MESH
BF = jnp.bfloat16
F32 = jnp.float32
NZ = 8
NT = (((1,), (1,)), ((), ()))
NN = (((1,), (0,)), ((), ()))


def cell_sums():
    main = np.zeros((3, 3, 4, 16, 8, 32), np.float32)
    edge = np.zeros((2, 3, 16, 8, 32), np.float32)
    for b in range(3):
        for e in range(3):
            for c in range(16):
                cols = [2 * c + q + 1 - e for q in range(2) if 0 <= 2 * c + q + 1 - e < 32]
                for h in range(4):
                    for p in range(2):
                        row = 2 * h + p + 1 - b
                        if 0 <= row < 8:
                            main[b, e, h, c, row, cols] = 1.0
                if b == 0:
                    edge[0, e, c, 0, cols] = 1.0
                if b == 2:
                    edge[1, e, c, 7, cols] = 1.0
    return np.concatenate([main.reshape(576, 256), edge.reshape(96, 256)], axis=0)


def tap_places():
    middle = [(1, e, a) for e in range(3) for a in range(3)]
    rest = [middle[8]] + [(b, e, a) for b in (0, 2) for e in range(3) for a in range(3)]
    places = []
    for x in range(4):
        places += middle[2 * x : 2 * x + 2] + rest[5 * x : 5 * x + 5]
    return places


def dot(a, b, dims):
    return lax.dot_general(a, b, dims, preferred_element_type=F32)


def body(
    scale,
    lat_in, og_in, wt_in, w2_in, sums_in, eye_in,
    gi_out, gw_out,
    xg, og, w, w2, g, gh, acc, ah, q, qh, pre, ga, es, er,
    act, gp3, act3, act3t, gi, pb, rp, ps, rr, gws, ra, sbf, sb, rb, fc, rc,
    loc_s, w2_s, ag_s, ag_r, wz_s, wz_r, wx_s, wx_r, e_s, e_r, pr_s, pr_r, rs_s, rs_r,
    a_s, a_r, b_s, b_r, c_s, c_r,
):
    x = lax.axis_index("dp")
    tm = lax.axis_index("tm")
    height = lax.axis_index("height")
    c = tm % 2
    ylo = tm // 2
    z = height % NZ
    yhi = height // NZ
    y = 2 * yhi + ylo
    y_out = 2 * ylo + yhi

    def dev(x_, y_, z_, c_):
        return (x_, (y_ % 2) * 2 + c_, (y_ // 2) * NZ + z_)

    up_y, down_y = (y + 1) % 4, (y + 3) % 4
    up_z, down_z = (z + 1) % NZ, (z + NZ - 1) % NZ
    up_x, down_x = (x + 1) % 4, (x + 3) % 4
    far_y, far_x = (y + 2) % 4, (x + 2) % 4

    def remote(src, dst, ssem, rsem, target):
        return pltpu.make_async_remote_copy(
            src_ref=src, dst_ref=dst, send_sem=ssem, recv_sem=rsem,
            device_id=target, device_id_type=MESH,
        )

    def slab(ref, y_, c_, f):
        return ref.at[2 * (2 * (y_ % 2) + c_) + f, y_ // 2]

    def block(ref, y_, c_):
        return ref.at[pl.ds(2 * (2 * (y_ % 2) + c_), 2), y_ // 2]

    pos = (z + NZ - (4 * c + 2 * ylo)) % NZ
    source = pos < 2
    base = 64 * (4 * yhi + 2 * c + ylo)
    own = [
        pltpu.make_async_copy(lat_in, block(xg, y, c), loc_s.at[0]),
        pltpu.make_async_copy(og_in, block(og, y, c), loc_s.at[1]),
    ]
    own_w = pltpu.make_async_copy(wt_in, w.at[:, pos % 2], loc_s.at[2])
    w2_copies = [
        pltpu.make_async_copy(
            w2_in.at[9 * a + k, pl.ds(pl.multiple_of(base, 64), 64)],
            w2.at[64 * a : 64 * a + 64, 256 * k : 256 * k + 256],
            w2_s.at[a, k],
        )
        for a in range(3)
        for k in range(9)
    ]

    @pl.when(source)
    def _():
        own_w.start()

    for copy in own:
        copy.start()

    barrier = pltpu.get_barrier_semaphore()

    def greet(target):
        pl.semaphore_signal(barrier, inc=1, device_id=target, device_id_type=MESH)

    greet(dev(x, y, z, 1 - c))
    for d in (1, 3, 2):
        greet(dev(x, (y + d) % 4, z, c))
        greet(dev((x + d) % 4, y, z, c))
    for d in (1, 7, 2, 6, 3, 5, 4):
        greet(dev(x, y, (z + d) % NZ, c))
    swaps = y != y_out

    @pl.when(swaps)
    def _():
        for d in range(1, 4):
            greet(dev((x + d) % 4, y_out, z, c))

    for copy in w2_copies:
        copy.start()
    acc[...] = jnp.zeros_like(acc)
    ah[...] = jnp.zeros_like(ah)

    @pl.when(source)
    def _():
        own_w.wait()

    for copy in own:
        copy.wait()
    pl.semaphore_wait(barrier, 14 + 3 * swaps.astype(jnp.int32))

    arrays = (og, xg)

    def gather(n, i):
        ref = arrays[n]
        up, down, mate = dev(x, up_y, z, c), dev(x, down_y, z, c), dev(x, y, z, 1 - c)
        place, target = {
            0: lambda: (slab(ref, y, c, 0), up),
            1: lambda: (slab(ref, y, c, 1), down),
            2: lambda: (slab(ref, y, c, 1), up),
            3: lambda: (slab(ref, y, c, 0), down),
            4: lambda: (block(ref, y, c), mate),
            5: lambda: (slab(ref, down_y, c, 0), up),
            6: lambda: (slab(ref, up_y, c, 1), down),
            7: lambda: (block(ref, down_y, c), mate),
            8: lambda: (block(ref, up_y, c), mate),
            9: lambda: (block(ref, far_y, c), mate),
        }[i]()
        return remote(place, place, ag_s.at[n, i], ag_r.at[n, i], target)

    reach = (4, 4, 3)

    def share(part, slot):
        if part < 2:
            return w.at[pl.ds(6 * x + 3 * part, 3), slot]
        return w.at[24:27, slot]

    def along_z(part, slot, way):
        step = (1, NZ - 1, 2, NZ - 2)[way]
        target = dev(x, y, (z + step) % NZ, c)
        place = share(part, slot)
        return remote(place, place, wz_s.at[part, slot, way], wz_r.at[part, slot], target)

    def z_sends(part, slot, act_on):
        far = (pos + NZ - slot) % NZ
        if part < 2:
            @pl.when(far < 3)
            def _():
                act_on(along_z(part, slot, 2))

            @pl.when(far == 0)
            def _():
                act_on(along_z(part, slot, 0))
                act_on(along_z(part, slot, 1))

            @pl.when(jnp.logical_or(far == 0, far == NZ - 1))
            def _():
                act_on(along_z(part, slot, 3))

            return
        r = reach[part]

        @pl.when(far < r)
        def _():
            act_on(along_z(part, slot, 0))

        @pl.when(jnp.logical_or(far == 0, far > r + 1))
        def _():
            act_on(along_z(part, slot, 1))

    def goes_on(part, slot):
        far = (pos + NZ - slot) % NZ
        r = reach[part]
        return jnp.logical_and(far != 0, jnp.logical_or(far < r, far > r + 1))

    def along_x(slot, i):
        up, down = dev(up_x, y, z, c), dev(down_x, y, z, c)
        first, target = (
            (6 * x, up), (6 * x + 3, up), (6 * x + 3, down), (6 * x, down),
            (6 * down_x, up), (6 * up_x + 3, down),
        )[i]
        place = w.at[pl.ds(first, 3), slot]
        return remote(place, place, wx_s.at[slot, i], wx_r.at[slot, i], target)

    def start(copy):
        copy.start()

    closer = jnp.where(jnp.logical_and(pos >= 1, pos <= 4), 1, 0)
    slots = (closer, 1 - closer)
    own_slot = pos % 2

    @pl.when(source)
    def _():
        z_sends(0, own_slot, start)
        z_sends(1, own_slot, start)

    for i in range(5):
        gather(0, i).start()

    @pl.when(source)
    def _():
        z_sends(2, own_slot, start)

    for i in range(5):
        gather(1, i).start()

    def pass_on(part, slot):
        @pl.when(pos != slot if part < 2 else goes_on(part, slot))
        def _():
            along_z(part, slot, 0).wait_recv()
            z_sends(part, slot, start)
            if part < 2:
                along_x(slot, part).start()
                along_x(slot, 3 - part).start()

    def pass_end(part, slot):
        @pl.when(jnp.logical_and(pos != slot, jnp.logical_not(goes_on(part, slot))))
        def _():
            along_z(part, slot, 0).wait_recv()

    def pass_x(slot):
        @pl.when(pos != slot)
        def _():
            along_x(slot, 0).wait_recv()
            along_x(slot, 4).start()
            along_x(slot, 2).wait_recv()
            along_x(slot, 5).start()

    def pass_y(n):
        gather(n, 0).wait_recv()
        gather(n, 5).start()
        gather(n, 1).wait_recv()
        gather(n, 6).start()

    def pass_mate(n):
        gather(n, 2).wait_recv()
        gather(n, 7).start()
        gather(n, 3).wait_recv()
        gather(n, 8).start()

    def pass_far(n):
        gather(n, 5).wait_recv()
        gather(n, 6).wait_recv()
        gather(n, 9).start()

    near, far = slots
    close = jnp.logical_or(pos < 3, pos == 7)

    def pass_z(*steps):
        for part, slot in steps:
            pass_on(part, slot)

    def sums_of(f, band):
        part = dot(sums_in[...], og[f, band], NN)
        for k in range(9):
            g[f, band, :, 256 * k : 256 * k + 256] = part[64 * k : 64 * k + 64].astype(BF)
        for k in range(6):
            lane = 256 * (k % 3)
            gh[k // 3, f, band, :, lane : lane + 256] = part[576 + 16 * k : 592 + 16 * k].astype(BF)

    def sums(core, half):
        def step(f, _):
            sums_of(4 * half + 2 * core + f, 0)
            sums_of(4 * half + 2 * core + f, 1)
            return 0

        lax.fori_loop(0, 2, step, 0)

    @pl.when(close)
    def _():
        pass_z((0, near), (1, near))
        pass_y(0)
        pass_z((0, far), (1, far))
        pass_z((2, near))
        pass_mate(0)
        pass_x(near)
        pass_z((2, far))
        pass_y(1)
        pass_far(0)
        pass_x(far)
        sums(c, 0)
        pass_mate(1)
        sums(c, 1)
        pass_far(1)

    @pl.when(jnp.logical_not(close))
    def _():
        pass_y(0)
        pass_z((0, near), (1, near))
        pass_mate(0)
        pass_z((0, far), (1, far))
        pass_y(1)
        pass_far(0)
        pass_x(near)
        pass_z((2, near))
        pass_mate(1)
        sums(c, 0)
        pass_x(far)
        pass_z((2, far))
        pass_far(1)
        sums(c, 1)

    for i in (4, 7, 8, 9):
        gather(0, i).wait_recv()
    sums(1 - c, 0)

    sums(1 - c, 1)
    for copy in w2_copies:
        copy.wait()

    def edge_copy(n, side):
        target = dev(x, y, down_z if side == 0 else up_z, c)
        return remote(es.at[n, side], er.at[n, side], e_s.at[n, side], e_r.at[n, side], target)

    def edge_send(n, rows):
        for side in range(2):
            for t in range(4):
                es[n, side, t] = jnp.concatenate([rows(side, t), rows(side, t + 4)], axis=-1).astype(BF)
            edge_copy(n, side).start()

    def edge_wait(n):
        for side in range(2):
            edge_copy(n, side).wait_recv()

    last, first = z == NZ - 1, z == 0

    def edge_rows(n, side, t):
        v = er[n, side, t % 4][:, :, 64 * (t // 4) : 64 * (t // 4) + 64].astype(F32)
        if side == 0:
            return jnp.where(last, jnp.stack([v[1], jnp.zeros_like(v[1])]), v)
        return jnp.where(first, jnp.stack([jnp.zeros_like(v[0]), v[0]]), v)

    def through_time(ref, t):
        out = ref[t, :, :, 128:192]
        if t < 7:
            out = out + ref[t + 1, :, :, 64:128]
        if t < 6:
            out = out + ref[t + 2, :, :, 0:64]
        return out

    for side in range(2):
        lanes = slice(1536 * side, 1536 * side + 768)
        qh[side] = dot(gh[side].reshape(256, 768), w2[:, lanes], NT).reshape(8, 2, 16, 192)
    edge_send(1, lambda side, t: through_time(qh.at[side], t))
    q[...] = dot(g[...].reshape(1024, 2304), w2[...], NT).reshape(8, 2, 64, 192)
    for t in range(8):
        ga[t] = through_time(q, t)

    for i in (4, 7, 8, 9):
        gather(1, i).wait_recv()
    for slot in range(2):
        pass_end(2, slot)

        @pl.when(pos != slot)
        def _():
            for i in (1, 3, 4, 5):
                along_x(slot, i).wait_recv()

    def summed_columns(part):
        rows = part.shape[0]
        col = lax.broadcasted_iota(jnp.int32, (rows, 64), 0) % 16
        before = jnp.where(col == 0, 0.0, pltpu.roll(part[:, 0:64], 1, 0))
        after = jnp.where(col == 15, 0.0, pltpu.roll(part[:, 128:192], rows - 1, 0))
        return before + part[:, 64:128] + after

    for side in range(2):
        for a in range(3):
            n = 6 + a
            k = 9 * a + 6 * (1 - side)
            rows = xg[0:n, :, 48 * side : 48 * side + 16].reshape(n * 32, 512)
            part = dot(rows, w[k : k + 3].reshape(192, 512), NT)
            ah[side, 2 - a : 8] += part.reshape(n, 2, 16, 192)
    edge_send(0, lambda side, t: summed_columns(ah[side, t].reshape(32, 192)).reshape(2, 16, 64))

    for a in range(3):
        n = 6 + a
        for b in range(3):
            k = 9 * a + 3 * b
            lo = 16 if b == 2 else 0
            to = 16 if b == 0 else 0
            size = 64 if b == 1 else 48
            rows = xg[0:n, :, lo : lo + size].reshape(n * 2 * size, 512)
            part = dot(rows, w[k : k + 3].reshape(192, 512), NT)
            acc[2 - a : 8, :, to : to + size, :] += part.reshape(n, 2, size, 192)

    def columns(t, _):
        pre[t, :, 16:80] = summed_columns(acc[t].reshape(128, 192)).reshape(2, 64, 64)
        return 0

    lax.fori_loop(0, 8, columns, 0)

    edge_wait(0)
    for t in range(8):
        pre[t, :, 16:32] += edge_rows(0, 1, t)
        pre[t, :, 64:80] += edge_rows(0, 0, t)
        v = pre[t, :, 16:80]
        s = 1.0 / (1.0 + jnp.exp(-v))
        act[t] = v * s
        pre[t, :, 16:80] = s * (1.0 + v * (1.0 - s))
    edge_send(2, lambda side, t: act[t, :, 48 * side : 48 * side + 16])

    def stacked(rows, t):
        v = rows(t)
        zero = jnp.zeros_like(v)
        return jnp.concatenate([rows(t - 2) if t > 1 else zero, rows(t - 1) if t > 0 else zero, v], axis=-1)

    for t in range(8):
        act3[t] = stacked(lambda u: act[u], t).astype(BF)
    act3t[...] = dot(eye_in[...], act3[...].reshape(1024, 192), NT).astype(BF)

    first_place, size = (0, 2, 6), (2, 4, 1)
    places = tap_places()

    def x_copy(d, i):
        to = (x + d) % 4
        lo = first_place[i]
        return remote(
            gws.at[pl.ds(7 * to + lo, size[i])], ra.at[d - 1, lo : lo + size[i]],
            a_s.at[d - 1, i], a_r.at[d - 1, i], dev(to, y, z, c),
        )

    def keep(b, part):
        for e in range(3):
            for a in range(3):
                gws[places.index((b, e, a))] = part[64 * a : 64 * a + 64, 256 * e : 256 * e + 256].astype(BF)

    def own_cells(b):
        return dot(act3t[...], g[:, :, :, 768 * b : 768 * b + 768].reshape(1024, 768), NN)

    keep(1, own_cells(1))
    for d in (2, 1, 3):
        x_copy(d, 0).start()

    edge_wait(1)
    for t in range(8):
        ga[t, :, 0:16] += edge_rows(1, 1, t)
        ga[t, :, 48:64] += edge_rows(1, 0, t)
        pre[t, :, 16:80] = ga[t] * pre[t, :, 16:80]
    edge_send(3, lambda side, t: pre[t, :, 16 + 48 * side : 32 + 48 * side])

    parts = (own_cells(0), own_cells(2))
    edge_wait(2)
    for t in range(8):
        for side in range(2):
            qh[side, t, :, :, 0:64] = edge_rows(2, 1 - side, t)
    for side in range(2):
        stack = jnp.concatenate(
            [stacked(lambda u: qh[side, u, :, :, 0:64], t).reshape(32, 192) for t in range(8)], axis=0
        ).astype(BF)
        hal3t = dot(eye_in[...], stack, NT).astype(BF)
        keep(2 * side, parts[side] + dot(hal3t, gh[side].reshape(256, 768), NN))
    gws[27] = jnp.zeros((64, 256), BF)
    for i in (1, 2):
        for d in (2, 1, 3):
            x_copy(d, i).start()

    edge_wait(3)
    for t in range(8):
        pre[t, :, 0:16] = edge_rows(3, 1, t)
        pre[t, :, 80:96] = edge_rows(3, 0, t)

    col96 = lax.broadcasted_iota(jnp.int32, (192, 64), 0) % 16

    def shifted(t, _):
        part = pre[t].reshape(192, 64)
        after = jnp.where(col96 == 15, 0.0, pltpu.roll(part, 191, 0))
        before = jnp.where(col96 == 0, 0.0, pltpu.roll(part, 1, 0))
        gp3[t] = jnp.concatenate([after, part, before], axis=-1).reshape(2, 96, 192).astype(BF)
        return 0

    lax.fori_loop(0, 8, shifted, 0)
    gi[...] = jnp.zeros_like(gi)
    for a in range(3):
        n = 6 + a
        for b in range(3):
            k = 9 * a + 3 * b
            rows = gp3[2 - a : 8, :, 16 * (2 - b) : 16 * (2 - b) + 64, :].reshape(n * 128, 192)
            part = dot(rows, w[k : k + 3].reshape(192, 512), NN)
            gi[0:n] += part.reshape(n, 2, 64, 512)

    for half in range(2):
        for f in range(2):
            pb[half, f] = gi[4 * half + 2 * (1 - c) + f].astype(BF)
    pair_copy = remote(pb, rp, pr_s, pr_r, dev(x, y, z, 1 - c))
    pair_copy.start()

    sbf[:, 56:64] = jnp.zeros((8, 8, 256), F32)

    def rows_of(i):
        return slice(8 * first_place[i], 8 * first_place[i] + max(8 * size[i], 16))

    def z_copy(d, i):
        to = (z + d) % NZ
        part = rows_of(i)
        return remote(sb.at[to, part], rb.at[d - 1, part], b_s.at[d - 1, i], b_r.at[d - 1, i], dev(x, y, to, c))

    def x_sum(i):
        for d in range(1, 4):
            x_copy(d, i).wait_recv()
        for j in range(first_place[i], first_place[i] + size[i]):
            total = gws[7 * x + j].astype(F32)
            for d in range(3):
                total = total + ra[d, j].astype(F32)
            sbf[:, 8 * j : 8 * j + 8] = total.reshape(8, 8, 256)
        part = rows_of(i)
        sb[:, part] = sbf[:, part].astype(BF)
        for d in (4, 3, 5, 2, 6, 1, 7):
            z_copy(d, i).start()

    def z_sum(i):
        part = rows_of(i)
        for d in range(1, NZ):
            z_copy(d, i).wait_recv()
        total = sb[z, part].astype(F32)
        for d in range(NZ - 1):
            total = total + rb[d, part].astype(F32)
        fc[part] = (total * scale).astype(BF)

    x_sum(0)
    pair_copy.wait_recv()
    for half in range(2):
        for f in range(2):
            ps[half, f] = (gi[4 * half + 2 * c + f] + rp[half, f].astype(F32)).astype(BF)

    def y_copy(d):
        to = (y + d) % 4
        return remote(ps.at[to % 2, :, to // 2], rr.at[d - 1], rs_s.at[d - 1], rs_r.at[d - 1], dev(x, to, z, c))

    for d in (2, 1, 3):
        y_copy(d).start()

    x_sum(1)
    z_sum(0)
    x_sum(2)
    z_sum(1)
    z_sum(2)

    def out_copy(to_x):
        return remote(fc, rc.at[x], c_s.at[to_x], c_r.at[x], dev(to_x, y_out, z, c))

    for to_x in range(4):
        mine = jnp.logical_and(x == to_x, y == y_out)

        @pl.when(mine)
        def _():
            pltpu.make_async_copy(fc, rc.at[x], c_r.at[x]).start()

        @pl.when(jnp.logical_not(mine))
        def _():
            out_copy(to_x).start()

    for d in range(1, 4):
        y_copy(d).wait_recv()
    total = ps[ylo, :, yhi].astype(F32)
    for d in range(3):
        total = total + rr[d].astype(F32)
    gi_out[...] = total.astype(BF)

    for part in range(4):
        pltpu.make_async_copy(fc, rc.at[part], c_r.at[part]).wait()
        v = rc[part].astype(F32)
        for j in range(7):
            if 7 * part + j < 27:
                b, e, a = places[7 * part + j]
                gw_out[9 * a + 3 * b + e] = v[8 * j : 8 * j + 8]

    def sent(copy):
        copy.wait_send()

    for n in range(2):
        for i in range(10):
            gather(n, i).wait_send()
    for part in range(3):
        for slot in range(2):
            z_sends(part, slot, sent)
    for slot in range(2):
        @pl.when(pos != slot)
        def _():
            for i in range(6):
                along_x(slot, i).wait_send()

    for n in range(4):
        for side in range(2):
            edge_copy(n, side).wait_send()
    pair_copy.wait_send()
    for d in range(1, 4):
        for i in range(3):
            x_copy(d, i).wait_send()
        y_copy(d).wait_send()
    for d in range(1, NZ):
        for i in range(3):
            z_copy(d, i).wait_send()
    for to_x in range(4):
        @pl.when(jnp.logical_not(jnp.logical_and(x == to_x, y == y_out)))
        def _():
            out_copy(to_x).wait_send()


def on_device(latent, out_grad, w_first, w_second):
    wt = jnp.swapaxes(w_first, 1, 2)
    scale = 1.0 / math.sqrt(131072.0)
    hbm = pl.BlockSpec(memory_space=pl.ANY)
    vmem = pl.BlockSpec(memory_space=pltpu.VMEM)
    dma = pltpu.SemaphoreType.DMA
    grad_input, grad_w2 = pl.pallas_call(
        functools.partial(body, scale),
        out_shape=(
            jax.ShapeDtypeStruct((2, 64, 512), BF),
            jax.ShapeDtypeStruct((27, 8, 256), F32),
        ),
        in_specs=[hbm, hbm, hbm, hbm, vmem, vmem],
        out_specs=(vmem, vmem),
        scratch_shapes=[
            pltpu.VMEM((8, 2, 64, 512), BF),
            pltpu.VMEM((8, 2, 256, 256), BF),
            pltpu.VMEM((27, 2, 32, 512), BF),
            pltpu.VMEM((192, 2304), BF),
            pltpu.VMEM((8, 2, 64, 2304), BF),
            pltpu.VMEM((2, 8, 2, 16, 768), BF),
            pltpu.VMEM((8, 2, 64, 192), F32),
            pltpu.VMEM((2, 8, 2, 16, 192), F32),
            pltpu.VMEM((8, 2, 64, 192), F32),
            pltpu.VMEM((2, 8, 2, 16, 192), F32),
            pltpu.VMEM((8, 2, 96, 64), F32),
            pltpu.VMEM((8, 2, 64, 64), F32),
            pltpu.VMEM((4, 2, 4, 2, 16, 128), BF),
            pltpu.VMEM((4, 2, 4, 2, 16, 128), BF),
            pltpu.VMEM((8, 2, 64, 64), F32),
            pltpu.VMEM((8, 2, 96, 192), BF),
            pltpu.VMEM((8, 2, 64, 192), BF),
            pltpu.VMEM((192, 1024), BF),
            pltpu.VMEM((8, 2, 64, 512), F32),
            pltpu.VMEM((2, 2, 2, 64, 512), BF),
            pltpu.VMEM((2, 2, 2, 64, 512), BF),
            pltpu.VMEM((2, 2, 2, 64, 512), BF),
            pltpu.VMEM((3, 2, 64, 512), BF),
            pltpu.VMEM((28, 64, 256), BF),
            pltpu.VMEM((3, 7, 64, 256), BF),
            pltpu.VMEM((8, 64, 256), F32),
            pltpu.VMEM((8, 64, 256), BF),
            pltpu.VMEM((7, 64, 256), BF),
            pltpu.VMEM((64, 256), BF),
            pltpu.VMEM((4, 64, 256), BF),
            dma((3,)), dma((3, 9)),
            dma((2, 10)), dma((2, 10)),
            dma((3, 2, 4)), dma((3, 2)),
            dma((2, 6)), dma((2, 6)),
            dma((4, 2)), dma((4, 2)),
            dma, dma,
            dma((3,)), dma((3,)),
            dma((3, 3)), dma((3, 3)),
            dma((7, 3)), dma((7, 3)),
            dma((4,)), dma((4,)),
        ],
        compiler_params=pltpu.CompilerParams(
            collective_id=0, has_side_effects=True, vmem_limit_bytes=56 * 1024 * 1024
        ),
    )(
        latent.reshape(2, 64, 512),
        out_grad.reshape(2, 256, 256),
        wt,
        w_second,
        jnp.asarray(cell_sums(), BF),
        jnp.asarray(np.eye(192, dtype=np.float32), BF),
    )
    return grad_input.reshape(1, 2, 4, 16, 512), jnp.swapaxes(grad_w2, 0, 1)


def solution(mesh):
    placed = (
        P("dp", "tm", "height", None, None),
        P("dp", "tm", "height", None, None),
        P(None, None, "height"),
        P(),
    )
    return jax.shard_map(
        on_device,
        mesh=mesh,
        in_specs=placed,
        out_specs=(P("dp", "tm", "height", None, None), P(("tm", "height"), None, None)),
        check_vma=False,
    )
```

```python
import functools
import math

import jax
import jax.numpy as jnp
import numpy as np
from jax import lax
from jax.experimental import pallas as pl
from jax.experimental.pallas import tpu as pltpu
from jax.sharding import PartitionSpec as P

MESH = pl.DeviceIdType.MESH
BF = jnp.bfloat16
F32 = jnp.float32
NZ = 8
NT = (((1,), (1,)), ((), ()))
NN = (((1,), (0,)), ((), ()))


def cell_sums():
    main = np.zeros((3, 3, 4, 16, 8, 32), np.float32)
    edge = np.zeros((2, 3, 16, 8, 32), np.float32)
    for b in range(3):
        for e in range(3):
            for c in range(16):
                cols = [2 * c + q + 1 - e for q in range(2) if 0 <= 2 * c + q + 1 - e < 32]
                for h in range(4):
                    for p in range(2):
                        row = 2 * h + p + 1 - b
                        if 0 <= row < 8:
                            main[b, e, h, c, row, cols] = 1.0
                if b == 0:
                    edge[0, e, c, 0, cols] = 1.0
                if b == 2:
                    edge[1, e, c, 7, cols] = 1.0
    return np.concatenate([main.reshape(576, 256), edge.reshape(96, 256)], axis=0)


def tap_places():
    middle = [(1, e, a) for e in range(3) for a in range(3)]
    rest = [middle[8]] + [(b, e, a) for b in (0, 2) for e in range(3) for a in range(3)]
    over_x = []
    for x in range(4):
        over_x += middle[2 * x : 2 * x + 2] + rest[3 * x : 3 * x + 3]
    return over_x, rest[12:]


def dot(a, b, dims):
    return lax.dot_general(a, b, dims, preferred_element_type=F32)


def body(
    scale,
    lat_in, og_in, wt_in, w2_in, sums_in, eye_in,
    gi_out, gw_out,
    xg, og, w, w2, g, gh, acc, ah, q, qh, pre, ga, es, er,
    act, gp3, act3, act3t, gi, pb, rp, ps, rr, gws, ra, sbf, sb, rb, fc, rc, zf, zs, rz, fz, rcz,
    loc_s, w2_s, ag_s, ag_r, wz_s, wz_r, wx_s, wx_r, e_s, e_r, pr_s, pr_r, rs_s, rs_r,
    a_s, a_r, b_s, b_r, c_s, c_r, d_s, d_r, f_s, f_r,
):
    x = lax.axis_index("dp")
    tm = lax.axis_index("tm")
    height = lax.axis_index("height")
    c = tm % 2
    ylo = tm // 2
    z = height % NZ
    yhi = height // NZ
    y = 2 * yhi + ylo
    y_out = 2 * ylo + yhi

    def dev(x_, y_, z_, c_):
        return (x_, (y_ % 2) * 2 + c_, (y_ // 2) * NZ + z_)

    up_y, down_y = (y + 1) % 4, (y + 3) % 4
    up_z, down_z = (z + 1) % NZ, (z + NZ - 1) % NZ
    up_x, down_x = (x + 1) % 4, (x + 3) % 4
    far_y, far_x = (y + 2) % 4, (x + 2) % 4

    def remote(src, dst, ssem, rsem, target):
        return pltpu.make_async_remote_copy(
            src_ref=src, dst_ref=dst, send_sem=ssem, recv_sem=rsem,
            device_id=target, device_id_type=MESH,
        )

    def slab(ref, y_, c_, f):
        return ref.at[2 * (2 * (y_ % 2) + c_) + f, y_ // 2]

    def block(ref, y_, c_):
        return ref.at[pl.ds(2 * (2 * (y_ % 2) + c_), 2), y_ // 2]

    pos = (z + NZ - (4 * c + 2 * ylo)) % NZ
    source = pos < 2
    base = 64 * (4 * yhi + 2 * c + ylo)
    own = [
        pltpu.make_async_copy(lat_in, block(xg, y, c), loc_s.at[0]),
        pltpu.make_async_copy(og_in, block(og, y, c), loc_s.at[1]),
    ]
    own_w = pltpu.make_async_copy(wt_in, w.at[:, pos % 2], loc_s.at[2])
    w2_copies = [
        pltpu.make_async_copy(
            w2_in.at[9 * a + k, pl.ds(pl.multiple_of(base, 64), 64)],
            w2.at[64 * a : 64 * a + 64, 256 * k : 256 * k + 256],
            w2_s.at[a, k],
        )
        for a in range(3)
        for k in range(9)
    ]

    @pl.when(source)
    def _():
        own_w.start()

    for copy in own:
        copy.start()

    barrier = pltpu.get_barrier_semaphore()

    def greet(target):
        pl.semaphore_signal(barrier, inc=1, device_id=target, device_id_type=MESH)

    greet(dev(x, y, z, 1 - c))
    for d in (1, 3, 2):
        greet(dev(x, (y + d) % 4, z, c))
        greet(dev((x + d) % 4, y, z, c))
    for d in (1, 7, 2, 6, 3, 5, 4):
        greet(dev(x, y, (z + d) % NZ, c))
    swaps = y != y_out

    @pl.when(swaps)
    def _():
        for d in range(1, 4):
            greet(dev((x + d) % 4, y_out, z, c))

    for copy in w2_copies:
        copy.start()
    acc[...] = jnp.zeros_like(acc)
    ah[...] = jnp.zeros_like(ah)

    @pl.when(source)
    def _():
        own_w.wait()

    for copy in own:
        copy.wait()
    pl.semaphore_wait(barrier, 14 + 3 * swaps.astype(jnp.int32))

    arrays = (og, xg)

    def gather(n, i):
        ref = arrays[n]
        up, down, mate = dev(x, up_y, z, c), dev(x, down_y, z, c), dev(x, y, z, 1 - c)
        place, target = {
            0: lambda: (slab(ref, y, c, 0), up),
            1: lambda: (slab(ref, y, c, 1), down),
            2: lambda: (slab(ref, y, c, 1), up),
            3: lambda: (slab(ref, y, c, 0), down),
            4: lambda: (block(ref, y, c), mate),
            5: lambda: (slab(ref, down_y, c, 0), up),
            6: lambda: (slab(ref, up_y, c, 1), down),
            7: lambda: (block(ref, down_y, c), mate),
            8: lambda: (block(ref, up_y, c), mate),
            9: lambda: (block(ref, far_y, c), mate),
        }[i]()
        return remote(place, place, ag_s.at[n, i], ag_r.at[n, i], target)

    reach = (4, 4, 3)

    def share(part, slot):
        if part < 2:
            return w.at[pl.ds(6 * x + 3 * part, 3), slot]
        return w.at[24:27, slot]

    def along_z(part, slot, way):
        step = (1, NZ - 1, 2, NZ - 2)[way]
        target = dev(x, y, (z + step) % NZ, c)
        place = share(part, slot)
        return remote(place, place, wz_s.at[part, slot, way], wz_r.at[part, slot], target)

    def z_sends(part, slot, act_on):
        far = (pos + NZ - slot) % NZ
        if part < 2:
            @pl.when(far < 3)
            def _():
                act_on(along_z(part, slot, 2))

            @pl.when(far == 0)
            def _():
                act_on(along_z(part, slot, 0))
                act_on(along_z(part, slot, 1))

            @pl.when(jnp.logical_or(far == 0, far == NZ - 1))
            def _():
                act_on(along_z(part, slot, 3))

            return
        r = reach[part]

        @pl.when(far < r)
        def _():
            act_on(along_z(part, slot, 0))

        @pl.when(jnp.logical_or(far == 0, far > r + 1))
        def _():
            act_on(along_z(part, slot, 1))

    def goes_on(part, slot):
        far = (pos + NZ - slot) % NZ
        r = reach[part]
        return jnp.logical_and(far != 0, jnp.logical_or(far < r, far > r + 1))

    def along_x(slot, i):
        up, down = dev(up_x, y, z, c), dev(down_x, y, z, c)
        first, target = (
            (6 * x, up), (6 * x + 3, up), (6 * x + 3, down), (6 * x, down),
            (6 * down_x, up), (6 * up_x + 3, down),
        )[i]
        place = w.at[pl.ds(first, 3), slot]
        return remote(place, place, wx_s.at[slot, i], wx_r.at[slot, i], target)

    def start(copy):
        copy.start()

    closer = jnp.where(jnp.logical_and(pos >= 1, pos <= 4), 1, 0)
    slots = (closer, 1 - closer)
    own_slot = pos % 2

    @pl.when(source)
    def _():
        z_sends(0, own_slot, start)
        z_sends(1, own_slot, start)

    for i in range(5):
        gather(0, i).start()

    @pl.when(source)
    def _():
        z_sends(2, own_slot, start)

    for i in range(5):
        gather(1, i).start()

    def pass_on(part, slot):
        @pl.when(pos != slot if part < 2 else goes_on(part, slot))
        def _():
            along_z(part, slot, 0).wait_recv()
            z_sends(part, slot, start)
            if part < 2:
                along_x(slot, part).start()
                along_x(slot, 3 - part).start()

    def pass_end(part, slot):
        @pl.when(jnp.logical_and(pos != slot, jnp.logical_not(goes_on(part, slot))))
        def _():
            along_z(part, slot, 0).wait_recv()

    def pass_x(slot):
        @pl.when(pos != slot)
        def _():
            along_x(slot, 0).wait_recv()
            along_x(slot, 4).start()
            along_x(slot, 2).wait_recv()
            along_x(slot, 5).start()

    def pass_y(n):
        gather(n, 0).wait_recv()
        gather(n, 5).start()
        gather(n, 1).wait_recv()
        gather(n, 6).start()

    def pass_mate(n):
        gather(n, 2).wait_recv()
        gather(n, 7).start()
        gather(n, 3).wait_recv()
        gather(n, 8).start()

    def pass_far(n):
        gather(n, 5).wait_recv()
        gather(n, 6).wait_recv()
        gather(n, 9).start()

    near, far = slots
    close = jnp.logical_or(pos < 3, pos == 7)

    def pass_z(*steps):
        for part, slot in steps:
            pass_on(part, slot)

    def sums_of(f, band):
        part = dot(sums_in[...], og[f, band], NN)
        for k in range(9):
            g[f, band, :, 256 * k : 256 * k + 256] = part[64 * k : 64 * k + 64].astype(BF)
        for k in range(6):
            lane = 256 * (k % 3)
            gh[k // 3, f, band, :, lane : lane + 256] = part[576 + 16 * k : 592 + 16 * k].astype(BF)

    def sums(core, half):
        def step(f, _):
            sums_of(4 * half + 2 * core + f, 0)
            sums_of(4 * half + 2 * core + f, 1)
            return 0

        lax.fori_loop(0, 2, step, 0)

    @pl.when(close)
    def _():
        pass_z((0, near), (1, near))
        pass_y(0)
        pass_z((0, far), (1, far))
        pass_z((2, near))
        pass_mate(0)
        pass_x(near)
        pass_z((2, far))
        pass_y(1)
        pass_far(0)
        pass_x(far)
        sums(c, 0)
        pass_mate(1)
        sums(c, 1)
        pass_far(1)

    @pl.when(jnp.logical_not(close))
    def _():
        pass_y(0)
        pass_z((0, near), (1, near))
        pass_mate(0)
        pass_z((0, far), (1, far))
        pass_y(1)
        pass_far(0)
        pass_x(near)
        pass_z((2, near))
        pass_mate(1)
        sums(c, 0)
        pass_x(far)
        pass_z((2, far))
        pass_far(1)
        sums(c, 1)

    for i in (4, 7, 8, 9):
        gather(0, i).wait_recv()
    sums(1 - c, 0)

    sums(1 - c, 1)
    for copy in w2_copies:
        copy.wait()

    def edge_copy(n, side):
        target = dev(x, y, down_z if side == 0 else up_z, c)
        return remote(es.at[n, side], er.at[n, side], e_s.at[n, side], e_r.at[n, side], target)

    def edge_send(n, rows):
        for side in range(2):
            for t in range(4):
                es[n, side, t] = jnp.concatenate([rows(side, t), rows(side, t + 4)], axis=-1).astype(BF)
            edge_copy(n, side).start()

    def edge_wait(n):
        for side in range(2):
            edge_copy(n, side).wait_recv()

    last, first = z == NZ - 1, z == 0

    def edge_rows(n, side, t):
        v = er[n, side, t % 4][:, :, 64 * (t // 4) : 64 * (t // 4) + 64].astype(F32)
        if side == 0:
            return jnp.where(last, jnp.stack([v[1], jnp.zeros_like(v[1])]), v)
        return jnp.where(first, jnp.stack([jnp.zeros_like(v[0]), v[0]]), v)

    def through_time(ref, t):
        out = ref[t, :, :, 128:192]
        if t < 7:
            out = out + ref[t + 1, :, :, 64:128]
        if t < 6:
            out = out + ref[t + 2, :, :, 0:64]
        return out

    for side in range(2):
        lanes = slice(1536 * side, 1536 * side + 768)
        qh[side] = dot(gh[side].reshape(256, 768), w2[:, lanes], NT).reshape(8, 2, 16, 192)
    edge_send(1, lambda side, t: through_time(qh.at[side], t))
    q[...] = dot(g[...].reshape(1024, 2304), w2[...], NT).reshape(8, 2, 64, 192)
    for t in range(8):
        ga[t] = through_time(q, t)

    for i in (4, 7, 8, 9):
        gather(1, i).wait_recv()
    for slot in range(2):
        pass_end(2, slot)

        @pl.when(pos != slot)
        def _():
            for i in (1, 3, 4, 5):
                along_x(slot, i).wait_recv()

    def summed_columns(part):
        rows = part.shape[0]
        col = lax.broadcasted_iota(jnp.int32, (rows, 64), 0) % 16
        before = jnp.where(col == 0, 0.0, pltpu.roll(part[:, 0:64], 1, 0))
        after = jnp.where(col == 15, 0.0, pltpu.roll(part[:, 128:192], rows - 1, 0))
        return before + part[:, 64:128] + after

    for side in range(2):
        for a in range(3):
            n = 6 + a
            k = 9 * a + 6 * (1 - side)
            rows = xg[0:n, :, 48 * side : 48 * side + 16].reshape(n * 32, 512)
            part = dot(rows, w[k : k + 3].reshape(192, 512), NT)
            ah[side, 2 - a : 8] += part.reshape(n, 2, 16, 192)
    edge_send(0, lambda side, t: summed_columns(ah[side, t].reshape(32, 192)).reshape(2, 16, 64))

    for a in range(3):
        n = 6 + a
        for b in range(3):
            k = 9 * a + 3 * b
            lo = 16 if b == 2 else 0
            to = 16 if b == 0 else 0
            size = 64 if b == 1 else 48
            rows = xg[0:n, :, lo : lo + size].reshape(n * 2 * size, 512)
            part = dot(rows, w[k : k + 3].reshape(192, 512), NT)
            acc[2 - a : 8, :, to : to + size, :] += part.reshape(n, 2, size, 192)

    def columns(t, _):
        pre[t, :, 16:80] = summed_columns(acc[t].reshape(128, 192)).reshape(2, 64, 64)
        return 0

    lax.fori_loop(0, 8, columns, 0)

    edge_wait(0)
    for t in range(8):
        pre[t, :, 16:32] += edge_rows(0, 1, t)
        pre[t, :, 64:80] += edge_rows(0, 0, t)
        v = pre[t, :, 16:80]
        s = 1.0 / (1.0 + jnp.exp(-v))
        act[t] = v * s
        pre[t, :, 16:80] = s * (1.0 + v * (1.0 - s))
    edge_send(2, lambda side, t: act[t, :, 48 * side : 48 * side + 16])

    def stacked(rows, t):
        v = rows(t)
        zero = jnp.zeros_like(v)
        return jnp.concatenate([rows(t - 2) if t > 1 else zero, rows(t - 1) if t > 0 else zero, v], axis=-1)

    for t in range(8):
        act3[t] = stacked(lambda u: act[u], t).astype(BF)
    act3t[...] = dot(eye_in[...], act3[...].reshape(1024, 192), NT).astype(BF)

    first_place, size = (0, 2), (2, 3)
    over_x, over_z = tap_places()

    def x_copy(d, i):
        to = (x + d) % 4
        lo = first_place[i]
        return remote(
            gws.at[pl.ds(5 * to + lo, size[i])], ra.at[d - 1, lo : lo + size[i]],
            a_s.at[d - 1, i], a_r.at[d - 1, i], dev(to, y, z, c),
        )

    def zz_copy(d):
        to = (z + d) % NZ
        return remote(zs.at[to], rz.at[d - 1], d_s.at[d - 1], d_r.at[d - 1], dev(x, y, to, c))

    def keep(b, part):
        for e in range(3):
            for a in range(3):
                tap = part[64 * a : 64 * a + 64, 256 * e : 256 * e + 256]
                if (b, e, a) in over_x:
                    gws[over_x.index((b, e, a))] = tap.astype(BF)
                else:
                    m = over_z.index((b, e, a))
                    zf[:, 8 * m : 8 * m + 8] = tap.reshape(8, 8, 256)

    def own_cells(b):
        return dot(act3t[...], g[:, :, :, 768 * b : 768 * b + 768].reshape(1024, 768), NN)

    keep(1, own_cells(1))
    for d in (2, 1, 3):
        x_copy(d, 0).start()

    edge_wait(1)
    for t in range(8):
        ga[t, :, 0:16] += edge_rows(1, 1, t)
        ga[t, :, 48:64] += edge_rows(1, 0, t)
        pre[t, :, 16:80] = ga[t] * pre[t, :, 16:80]
    edge_send(3, lambda side, t: pre[t, :, 16 + 48 * side : 32 + 48 * side])

    parts = (own_cells(0), own_cells(2))
    edge_wait(2)
    for t in range(8):
        for side in range(2):
            qh[side, t, :, :, 0:64] = edge_rows(2, 1 - side, t)
    for side in range(2):
        stack = jnp.concatenate(
            [stacked(lambda u: qh[side, u, :, :, 0:64], t).reshape(32, 192) for t in range(8)], axis=0
        ).astype(BF)
        hal3t = dot(eye_in[...], stack, NT).astype(BF)
        keep(2 * side, parts[side] + dot(hal3t, gh[side].reshape(256, 768), NN))
    for d in (2, 1, 3):
        x_copy(d, 1).start()
    zf[:, 56:64] = jnp.zeros((8, 8, 256), F32)
    zs[...] = zf[...].astype(BF)
    for d in (4, 3, 5, 2, 6, 1, 7):
        zz_copy(d).start()

    edge_wait(3)
    for t in range(8):
        pre[t, :, 0:16] = edge_rows(3, 1, t)
        pre[t, :, 80:96] = edge_rows(3, 0, t)

    col96 = lax.broadcasted_iota(jnp.int32, (192, 64), 0) % 16

    def shifted(t, _):
        part = pre[t].reshape(192, 64)
        after = jnp.where(col96 == 15, 0.0, pltpu.roll(part, 191, 0))
        before = jnp.where(col96 == 0, 0.0, pltpu.roll(part, 1, 0))
        gp3[t] = jnp.concatenate([after, part, before], axis=-1).reshape(2, 96, 192).astype(BF)
        return 0

    lax.fori_loop(0, 8, shifted, 0)
    gi[...] = jnp.zeros_like(gi)
    for a in range(3):
        n = 6 + a
        for b in range(3):
            k = 9 * a + 3 * b
            rows = gp3[2 - a : 8, :, 16 * (2 - b) : 16 * (2 - b) + 64, :].reshape(n * 128, 192)
            part = dot(rows, w[k : k + 3].reshape(192, 512), NN)
            gi[0:n] += part.reshape(n, 2, 64, 512)

    for half in range(2):
        for f in range(2):
            pb[half, f] = gi[4 * half + 2 * (1 - c) + f].astype(BF)
    pair_copy = remote(pb, rp, pr_s, pr_r, dev(x, y, z, 1 - c))
    pair_copy.start()

    sbf[:, 40:48] = jnp.zeros((8, 8, 256), F32)

    def rows_of(i):
        return slice(16 * i, 16 + 32 * i)

    def z_copy(d, i):
        to = (z + d) % NZ
        part = rows_of(i)
        return remote(sb.at[to, part], rb.at[d - 1, part], b_s.at[d - 1, i], b_r.at[d - 1, i], dev(x, y, to, c))

    def x_sum(i):
        for d in range(1, 4):
            x_copy(d, i).wait_recv()
        for j in range(first_place[i], first_place[i] + size[i]):
            total = gws[5 * x + j].astype(F32)
            for d in range(3):
                total = total + ra[d, j].astype(F32)
            sbf[:, 8 * j : 8 * j + 8] = total.reshape(8, 8, 256)
        part = rows_of(i)
        sb[:, part] = sbf[:, part].astype(BF)
        for d in (4, 3, 5, 2, 6, 1, 7):
            z_copy(d, i).start()

    def z_sum(i):
        part = rows_of(i)
        for d in range(1, NZ):
            z_copy(d, i).wait_recv()
        total = sb[z, part].astype(F32)
        for d in range(NZ - 1):
            total = total + rb[d, part].astype(F32)
        fc[part] = (total * scale).astype(BF)

    x_sum(0)
    pair_copy.wait_recv()
    for half in range(2):
        for f in range(2):
            ps[half, f] = (gi[4 * half + 2 * c + f] + rp[half, f].astype(F32)).astype(BF)

    def y_copy(d):
        to = (y + d) % 4
        return remote(ps.at[to % 2, :, to // 2], rr.at[d - 1], rs_s.at[d - 1], rs_r.at[d - 1], dev(x, to, z, c))

    for d in (2, 1, 3):
        y_copy(d).start()

    for d in range(1, NZ):
        zz_copy(d).wait_recv()
    total = zs[z].astype(F32)
    for d in range(NZ - 1):
        total = total + rz[d].astype(F32)
    fz[...] = (total * scale).astype(BF)

    def mine(to_x):
        return jnp.logical_and(x == to_x, y == y_out)

    def out_z(to_x):
        return remote(fz, rcz.at[x], f_s.at[to_x], f_r.at[x], dev(to_x, y_out, z, c))

    for to_x in range(4):
        @pl.when(mine(to_x))
        def _():
            pltpu.make_async_copy(fz, rcz.at[x], f_r.at[x]).start()

        @pl.when(jnp.logical_not(mine(to_x)))
        def _():
            out_z(to_x).start()

    x_sum(1)
    z_sum(0)
    z_sum(1)

    def out_copy(to_x):
        return remote(fc, rc.at[x], c_s.at[to_x], c_r.at[x], dev(to_x, y_out, z, c))

    for to_x in range(4):
        @pl.when(mine(to_x))
        def _():
            pltpu.make_async_copy(fc, rc.at[x], c_r.at[x]).start()

        @pl.when(jnp.logical_not(mine(to_x)))
        def _():
            out_copy(to_x).start()

    for d in range(1, 4):
        y_copy(d).wait_recv()
    total = ps[ylo, :, yhi].astype(F32)
    for d in range(3):
        total = total + rr[d].astype(F32)
    gi_out[...] = total.astype(BF)

    total = None
    for part in range(4):
        pltpu.make_async_copy(fz, rcz.at[part], f_r.at[part]).wait()
        v = rcz[part].astype(F32)
        total = v if total is None else total + v
    for m, (b, e, a) in enumerate(over_z):
        gw_out[9 * a + 3 * b + e] = total[8 * m : 8 * m + 8]
    for part in range(4):
        pltpu.make_async_copy(fc, rc.at[part], c_r.at[part]).wait()
        v = rc[part].astype(F32)
        for j in range(5):
            b, e, a = over_x[5 * part + j]
            gw_out[9 * a + 3 * b + e] = v[8 * j : 8 * j + 8]

    def sent(copy):
        copy.wait_send()

    for n in range(2):
        for i in range(10):
            gather(n, i).wait_send()
    for part in range(3):
        for slot in range(2):
            z_sends(part, slot, sent)
    for slot in range(2):
        @pl.when(pos != slot)
        def _():
            for i in range(6):
                along_x(slot, i).wait_send()

    for n in range(4):
        for side in range(2):
            edge_copy(n, side).wait_send()
    pair_copy.wait_send()
    for d in range(1, 4):
        for i in range(2):
            x_copy(d, i).wait_send()
        y_copy(d).wait_send()
    for d in range(1, NZ):
        zz_copy(d).wait_send()
        for i in range(2):
            z_copy(d, i).wait_send()
    for to_x in range(4):
        @pl.when(jnp.logical_not(mine(to_x)))
        def _():
            out_copy(to_x).wait_send()
            out_z(to_x).wait_send()


def on_device(latent, out_grad, w_first, w_second):
    wt = jnp.swapaxes(w_first, 1, 2)
    scale = 1.0 / math.sqrt(131072.0)
    hbm = pl.BlockSpec(memory_space=pl.ANY)
    vmem = pl.BlockSpec(memory_space=pltpu.VMEM)
    dma = pltpu.SemaphoreType.DMA
    grad_input, grad_w2 = pl.pallas_call(
        functools.partial(body, scale),
        out_shape=(
            jax.ShapeDtypeStruct((2, 64, 512), BF),
            jax.ShapeDtypeStruct((27, 8, 256), F32),
        ),
        in_specs=[hbm, hbm, hbm, hbm, vmem, vmem],
        out_specs=(vmem, vmem),
        scratch_shapes=[
            pltpu.VMEM((8, 2, 64, 512), BF),
            pltpu.VMEM((8, 2, 256, 256), BF),
            pltpu.VMEM((27, 2, 32, 512), BF),
            pltpu.VMEM((192, 2304), BF),
            pltpu.VMEM((8, 2, 64, 2304), BF),
            pltpu.VMEM((2, 8, 2, 16, 768), BF),
            pltpu.VMEM((8, 2, 64, 192), F32),
            pltpu.VMEM((2, 8, 2, 16, 192), F32),
            pltpu.VMEM((8, 2, 64, 192), F32),
            pltpu.VMEM((2, 8, 2, 16, 192), F32),
            pltpu.VMEM((8, 2, 96, 64), F32),
            pltpu.VMEM((8, 2, 64, 64), F32),
            pltpu.VMEM((4, 2, 4, 2, 16, 128), BF),
            pltpu.VMEM((4, 2, 4, 2, 16, 128), BF),
            pltpu.VMEM((8, 2, 64, 64), F32),
            pltpu.VMEM((8, 2, 96, 192), BF),
            pltpu.VMEM((8, 2, 64, 192), BF),
            pltpu.VMEM((192, 1024), BF),
            pltpu.VMEM((8, 2, 64, 512), F32),
            pltpu.VMEM((2, 2, 2, 64, 512), BF),
            pltpu.VMEM((2, 2, 2, 64, 512), BF),
            pltpu.VMEM((2, 2, 2, 64, 512), BF),
            pltpu.VMEM((3, 2, 64, 512), BF),
            pltpu.VMEM((20, 64, 256), BF),
            pltpu.VMEM((3, 5, 64, 256), BF),
            pltpu.VMEM((8, 48, 256), F32),
            pltpu.VMEM((8, 48, 256), BF),
            pltpu.VMEM((7, 48, 256), BF),
            pltpu.VMEM((48, 256), BF),
            pltpu.VMEM((4, 48, 256), BF),
            pltpu.VMEM((8, 64, 256), F32),
            pltpu.VMEM((8, 64, 256), BF),
            pltpu.VMEM((7, 64, 256), BF),
            pltpu.VMEM((64, 256), BF),
            pltpu.VMEM((4, 64, 256), BF),
            dma((3,)), dma((3, 9)),
            dma((2, 10)), dma((2, 10)),
            dma((3, 2, 4)), dma((3, 2)),
            dma((2, 6)), dma((2, 6)),
            dma((4, 2)), dma((4, 2)),
            dma, dma,
            dma((3,)), dma((3,)),
            dma((3, 2)), dma((3, 2)),
            dma((7, 2)), dma((7, 2)),
            dma((4,)), dma((4,)),
            dma((7,)), dma((7,)),
            dma((4,)), dma((4,)),
        ],
        compiler_params=pltpu.CompilerParams(
            collective_id=0, has_side_effects=True, vmem_limit_bytes=56 * 1024 * 1024
        ),
    )(
        latent.reshape(2, 64, 512),
        out_grad.reshape(2, 256, 256),
        wt,
        w_second,
        jnp.asarray(cell_sums(), BF),
        jnp.asarray(np.eye(192, dtype=np.float32), BF),
    )
    return grad_input.reshape(1, 2, 4, 16, 512), jnp.swapaxes(grad_w2, 0, 1)


def solution(mesh):
    placed = (
        P("dp", "tm", "height", None, None),
        P("dp", "tm", "height", None, None),
        P(None, None, "height"),
        P(),
    )
    return jax.shard_map(
        on_device,
        mesh=mesh,
        in_specs=placed,
        out_specs=(P("dp", "tm", "height", None, None), P(("tm", "height"), None, None)),
        check_vma=False,
    )
```

```python
import functools
import math

import jax
import jax.numpy as jnp
import numpy as np
from jax import lax
from jax.experimental import pallas as pl
from jax.experimental.pallas import tpu as pltpu
from jax.sharding import PartitionSpec as P

MESH = pl.DeviceIdType.MESH
BF = jnp.bfloat16
F32 = jnp.float32
NZ = 8
NT = (((1,), (1,)), ((), ()))
NN = (((1,), (0,)), ((), ()))


def cell_sums():
    main = np.zeros((3, 3, 4, 16, 8, 32), np.float32)
    edge = np.zeros((2, 3, 16, 8, 32), np.float32)
    for b in range(3):
        for e in range(3):
            for c in range(16):
                cols = [2 * c + q + 1 - e for q in range(2) if 0 <= 2 * c + q + 1 - e < 32]
                for h in range(4):
                    for p in range(2):
                        row = 2 * h + p + 1 - b
                        if 0 <= row < 8:
                            main[b, e, h, c, row, cols] = 1.0
                if b == 0:
                    edge[0, e, c, 0, cols] = 1.0
                if b == 2:
                    edge[1, e, c, 7, cols] = 1.0
    return np.concatenate([main.reshape(576, 256), edge.reshape(96, 256)], axis=0)


def tap_places():
    middle = [(1, e, a) for e in range(3) for a in range(3)]
    rest = [middle[8]] + [(b, e, a) for b in (0, 2) for e in range(3) for a in range(3)]
    over_x = []
    for x in range(4):
        over_x += middle[2 * x : 2 * x + 2] + rest[3 * x : 3 * x + 3]
    return over_x, rest[12:]


def dot(a, b, dims):
    return lax.dot_general(a, b, dims, preferred_element_type=F32)


def body(
    scale,
    lat_in, og_in, wt_in, w2_in, sums_in, eye_in,
    gi_out, gw_out,
    xg, og, w, w2, g, gh, acc, ah, q, qh, pre, ga, es, er,
    act, gp3, act3, act3t, gi, pb, rp, ps, rr, gws, ra, sbf, sb, rb, fc, rc, zf, zs, rz, fz, rcz,
    loc_s, w2_s, ag_s, ag_r, wz_s, wz_r, wx_s, wx_r, e_s, e_r, pr_s, pr_r, rs_s, rs_r,
    a_s, a_r, b_s, b_r, c_s, c_r, d_s, d_r, f_s, f_r,
):
    x = lax.axis_index("dp")
    tm = lax.axis_index("tm")
    height = lax.axis_index("height")
    c = tm % 2
    ylo = tm // 2
    z = height % NZ
    yhi = height // NZ
    y = 2 * yhi + ylo
    y_out = 2 * ylo + yhi

    def dev(x_, y_, z_, c_):
        return (x_, (y_ % 2) * 2 + c_, (y_ // 2) * NZ + z_)

    up_y, down_y = (y + 1) % 4, (y + 3) % 4
    up_z, down_z = (z + 1) % NZ, (z + NZ - 1) % NZ
    up_x, down_x = (x + 1) % 4, (x + 3) % 4
    far_y, far_x = (y + 2) % 4, (x + 2) % 4

    def remote(src, dst, ssem, rsem, target):
        return pltpu.make_async_remote_copy(
            src_ref=src, dst_ref=dst, send_sem=ssem, recv_sem=rsem,
            device_id=target, device_id_type=MESH,
        )

    def slab(ref, y_, c_, f):
        return ref.at[2 * (2 * (y_ % 2) + c_) + f, y_ // 2]

    def block(ref, y_, c_):
        return ref.at[pl.ds(2 * (2 * (y_ % 2) + c_), 2), y_ // 2]

    pos = (z + NZ - (4 * c + 2 * ylo)) % NZ
    source = pos < 2
    base = 64 * (4 * yhi + 2 * c + ylo)
    own = [
        pltpu.make_async_copy(lat_in, block(xg, y, c), loc_s.at[0]),
        pltpu.make_async_copy(og_in, block(og, y, c), loc_s.at[1]),
    ]
    own_w = pltpu.make_async_copy(wt_in, w.at[:, pos % 2], loc_s.at[2])
    w2_copies = [
        pltpu.make_async_copy(
            w2_in.at[9 * a + k, pl.ds(pl.multiple_of(base, 64), 64)],
            w2.at[64 * a : 64 * a + 64, 256 * k : 256 * k + 256],
            w2_s.at[a, k],
        )
        for a in range(3)
        for k in range(9)
    ]

    @pl.when(source)
    def _():
        own_w.start()

    for copy in own:
        copy.start()

    barrier = pltpu.get_barrier_semaphore()

    def greet(target):
        pl.semaphore_signal(barrier, inc=1, device_id=target, device_id_type=MESH)

    greet(dev(x, y, z, 1 - c))
    for d in (1, 3, 2):
        greet(dev(x, (y + d) % 4, z, c))
        greet(dev((x + d) % 4, y, z, c))
    for d in (1, 7, 2, 6, 3, 5, 4):
        greet(dev(x, y, (z + d) % NZ, c))
    swaps = y != y_out

    @pl.when(swaps)
    def _():
        for d in range(1, 4):
            greet(dev((x + d) % 4, y_out, z, c))

    for copy in w2_copies:
        copy.start()
    acc[...] = jnp.zeros_like(acc)
    ah[...] = jnp.zeros_like(ah)

    @pl.when(source)
    def _():
        own_w.wait()

    for copy in own:
        copy.wait()
    pl.semaphore_wait(barrier, 14 + 3 * swaps.astype(jnp.int32))

    arrays = (og, xg)

    def gather(n, i):
        ref = arrays[n]
        up, down, mate = dev(x, up_y, z, c), dev(x, down_y, z, c), dev(x, y, z, 1 - c)
        place, target = {
            0: lambda: (slab(ref, y, c, 0), up),
            1: lambda: (slab(ref, y, c, 1), down),
            2: lambda: (slab(ref, y, c, 1), up),
            3: lambda: (slab(ref, y, c, 0), down),
            4: lambda: (block(ref, y, c), mate),
            5: lambda: (slab(ref, down_y, c, 0), up),
            6: lambda: (slab(ref, up_y, c, 1), down),
            7: lambda: (block(ref, down_y, c), mate),
            8: lambda: (block(ref, up_y, c), mate),
            9: lambda: (block(ref, far_y, c), mate),
        }[i]()
        return remote(place, place, ag_s.at[n, i], ag_r.at[n, i], target)

    reach = (4, 4, 3)

    def share(part, slot):
        if part < 2:
            return w.at[pl.ds(6 * x + 3 * part, 3), slot]
        return w.at[24:27, slot]

    def along_z(part, slot, way):
        step = (1, NZ - 1, 2, NZ - 2)[way]
        target = dev(x, y, (z + step) % NZ, c)
        place = share(part, slot)
        return remote(place, place, wz_s.at[part, slot, way], wz_r.at[part, slot], target)

    def z_sends(part, slot, act_on):
        far = (pos + NZ - slot) % NZ
        if part < 2:
            @pl.when(far < 3)
            def _():
                act_on(along_z(part, slot, 2))

            @pl.when(far == 0)
            def _():
                act_on(along_z(part, slot, 0))
                act_on(along_z(part, slot, 1))

            @pl.when(jnp.logical_or(far == 0, far == NZ - 1))
            def _():
                act_on(along_z(part, slot, 3))

            return
        r = reach[part]

        @pl.when(far < r)
        def _():
            act_on(along_z(part, slot, 0))

        @pl.when(jnp.logical_or(far == 0, far > r + 1))
        def _():
            act_on(along_z(part, slot, 1))

    def goes_on(part, slot):
        far = (pos + NZ - slot) % NZ
        r = reach[part]
        return jnp.logical_and(far != 0, jnp.logical_or(far < r, far > r + 1))

    def along_x(slot, i):
        up, down = dev(up_x, y, z, c), dev(down_x, y, z, c)
        first, target = (
            (6 * x, up), (6 * x + 3, up), (6 * x + 3, down), (6 * x, down),
            (6 * down_x, up), (6 * up_x + 3, down),
        )[i]
        place = w.at[pl.ds(first, 3), slot]
        return remote(place, place, wx_s.at[slot, i], wx_r.at[slot, i], target)

    def start(copy):
        copy.start()

    closer = jnp.where(jnp.logical_and(pos >= 1, pos <= 4), 1, 0)
    slots = (closer, 1 - closer)
    own_slot = pos % 2

    for i in range(5):
        gather(0, i).start()

    @pl.when(source)
    def _():
        z_sends(0, own_slot, start)
        z_sends(1, own_slot, start)


    @pl.when(source)
    def _():
        z_sends(2, own_slot, start)

    for i in range(5):
        gather(1, i).start()

    def pass_on(part, slot):
        @pl.when(pos != slot if part < 2 else goes_on(part, slot))
        def _():
            along_z(part, slot, 0).wait_recv()
            z_sends(part, slot, start)
            if part < 2:
                along_x(slot, part).start()
                along_x(slot, 3 - part).start()

    def pass_end(part, slot):
        @pl.when(jnp.logical_and(pos != slot, jnp.logical_not(goes_on(part, slot))))
        def _():
            along_z(part, slot, 0).wait_recv()

    def pass_x(slot):
        @pl.when(pos != slot)
        def _():
            along_x(slot, 0).wait_recv()
            along_x(slot, 4).start()
            along_x(slot, 2).wait_recv()
            along_x(slot, 5).start()

    def pass_y(n):
        gather(n, 0).wait_recv()
        gather(n, 5).start()
        gather(n, 1).wait_recv()
        gather(n, 6).start()

    def pass_mate(n):
        gather(n, 2).wait_recv()
        gather(n, 7).start()
        gather(n, 3).wait_recv()
        gather(n, 8).start()

    def pass_far(n):
        gather(n, 5).wait_recv()
        gather(n, 6).wait_recv()
        gather(n, 9).start()

    near, far = slots
    close = jnp.logical_or(pos < 3, pos == 7)

    def pass_z(*steps):
        for part, slot in steps:
            pass_on(part, slot)

    def sums_of(f, band):
        part = dot(sums_in[...], og[f, band], NN)
        for k in range(9):
            g[f, band, :, 256 * k : 256 * k + 256] = part[64 * k : 64 * k + 64].astype(BF)
        for k in range(6):
            lane = 256 * (k % 3)
            gh[k // 3, f, band, :, lane : lane + 256] = part[576 + 16 * k : 592 + 16 * k].astype(BF)

    def sums(core, half):
        def step(f, _):
            sums_of(4 * half + 2 * core + f, 0)
            sums_of(4 * half + 2 * core + f, 1)
            return 0

        lax.fori_loop(0, 2, step, 0)

    @pl.when(close)
    def _():
        pass_z((0, near), (1, near))
        pass_y(0)
        pass_z((0, far), (1, far))
        pass_z((2, near))
        pass_mate(0)
        pass_x(near)
        pass_z((2, far))
        pass_y(1)
        pass_far(0)
        pass_x(far)
        sums(c, 0)
        pass_mate(1)
        sums(c, 1)
        pass_far(1)

    @pl.when(jnp.logical_not(close))
    def _():
        pass_y(0)
        pass_z((0, near), (1, near))
        pass_mate(0)
        pass_z((0, far), (1, far))
        pass_y(1)
        pass_far(0)
        pass_x(near)
        pass_z((2, near))
        pass_mate(1)
        sums(c, 0)
        pass_x(far)
        pass_z((2, far))
        pass_far(1)
        sums(c, 1)

    for i in (4, 7, 8, 9):
        gather(0, i).wait_recv()
    sums(1 - c, 0)

    sums(1 - c, 1)
    for copy in w2_copies:
        copy.wait()

    def edge_copy(n, side):
        target = dev(x, y, down_z if side == 0 else up_z, c)
        return remote(es.at[n, side], er.at[n, side], e_s.at[n, side], e_r.at[n, side], target)

    def edge_send(n, rows):
        for side in range(2):
            for t in range(4):
                es[n, side, t] = jnp.concatenate([rows(side, t), rows(side, t + 4)], axis=-1).astype(BF)
            edge_copy(n, side).start()

    def edge_wait(n):
        for side in range(2):
            edge_copy(n, side).wait_recv()

    last, first = z == NZ - 1, z == 0

    def edge_rows(n, side, t):
        v = er[n, side, t % 4][:, :, 64 * (t // 4) : 64 * (t // 4) + 64].astype(F32)
        if side == 0:
            return jnp.where(last, jnp.stack([v[1], jnp.zeros_like(v[1])]), v)
        return jnp.where(first, jnp.stack([jnp.zeros_like(v[0]), v[0]]), v)

    def through_time(ref, t):
        out = ref[t, :, :, 128:192]
        if t < 7:
            out = out + ref[t + 1, :, :, 64:128]
        if t < 6:
            out = out + ref[t + 2, :, :, 0:64]
        return out

    for side in range(2):
        lanes = slice(1536 * side, 1536 * side + 768)
        qh[side] = dot(gh[side].reshape(256, 768), w2[:, lanes], NT).reshape(8, 2, 16, 192)
    edge_send(1, lambda side, t: through_time(qh.at[side], t))
    q[...] = dot(g[...].reshape(1024, 2304), w2[...], NT).reshape(8, 2, 64, 192)
    for t in range(8):
        ga[t] = through_time(q, t)

    for i in (4, 7, 8, 9):
        gather(1, i).wait_recv()
    for slot in range(2):
        pass_end(2, slot)

        @pl.when(pos != slot)
        def _():
            for i in (1, 3, 4, 5):
                along_x(slot, i).wait_recv()

    def summed_columns(part):
        rows = part.shape[0]
        col = lax.broadcasted_iota(jnp.int32, (rows, 64), 0) % 16
        before = jnp.where(col == 0, 0.0, pltpu.roll(part[:, 0:64], 1, 0))
        after = jnp.where(col == 15, 0.0, pltpu.roll(part[:, 128:192], rows - 1, 0))
        return before + part[:, 64:128] + after

    for side in range(2):
        for a in range(3):
            n = 6 + a
            k = 9 * a + 6 * (1 - side)
            rows = xg[0:n, :, 48 * side : 48 * side + 16].reshape(n * 32, 512)
            part = dot(rows, w[k : k + 3].reshape(192, 512), NT)
            ah[side, 2 - a : 8] += part.reshape(n, 2, 16, 192)
    edge_send(0, lambda side, t: summed_columns(ah[side, t].reshape(32, 192)).reshape(2, 16, 64))

    for a in range(3):
        n = 6 + a
        for b in range(3):
            k = 9 * a + 3 * b
            lo = 16 if b == 2 else 0
            to = 16 if b == 0 else 0
            size = 64 if b == 1 else 48
            rows = xg[0:n, :, lo : lo + size].reshape(n * 2 * size, 512)
            part = dot(rows, w[k : k + 3].reshape(192, 512), NT)
            acc[2 - a : 8, :, to : to + size, :] += part.reshape(n, 2, size, 192)

    def columns(t, _):
        pre[t, :, 16:80] = summed_columns(acc[t].reshape(128, 192)).reshape(2, 64, 64)
        return 0

    lax.fori_loop(0, 8, columns, 0)

    edge_wait(0)
    for t in range(8):
        pre[t, :, 16:32] += edge_rows(0, 1, t)
        pre[t, :, 64:80] += edge_rows(0, 0, t)
        v = pre[t, :, 16:80]
        s = 1.0 / (1.0 + jnp.exp(-v))
        act[t] = v * s
        pre[t, :, 16:80] = s * (1.0 + v * (1.0 - s))
    edge_send(2, lambda side, t: act[t, :, 48 * side : 48 * side + 16])

    def stacked(rows, t):
        v = rows(t)
        zero = jnp.zeros_like(v)
        return jnp.concatenate([rows(t - 2) if t > 1 else zero, rows(t - 1) if t > 0 else zero, v], axis=-1)

    for t in range(8):
        act3[t] = stacked(lambda u: act[u], t).astype(BF)
    act3t[...] = dot(eye_in[...], act3[...].reshape(1024, 192), NT).astype(BF)

    first_place, size = (0, 2), (2, 3)
    over_x, over_z = tap_places()

    def x_copy(d, i):
        to = (x + d) % 4
        lo = first_place[i]
        return remote(
            gws.at[pl.ds(5 * to + lo, size[i])], ra.at[d - 1, lo : lo + size[i]],
            a_s.at[d - 1, i], a_r.at[d - 1, i], dev(to, y, z, c),
        )

    def zz_copy(d):
        to = (z + d) % NZ
        return remote(zs.at[to], rz.at[d - 1], d_s.at[d - 1], d_r.at[d - 1], dev(x, y, to, c))

    def keep(b, part):
        for e in range(3):
            for a in range(3):
                tap = part[64 * a : 64 * a + 64, 256 * e : 256 * e + 256]
                if (b, e, a) in over_x:
                    gws[over_x.index((b, e, a))] = tap.astype(BF)
                else:
                    m = over_z.index((b, e, a))
                    zf[:, 8 * m : 8 * m + 8] = tap.reshape(8, 8, 256)

    def own_cells(b):
        return dot(act3t[...], g[:, :, :, 768 * b : 768 * b + 768].reshape(1024, 768), NN)

    keep(1, own_cells(1))
    for d in (2, 1, 3):
        x_copy(d, 0).start()

    edge_wait(1)
    for t in range(8):
        ga[t, :, 0:16] += edge_rows(1, 1, t)
        ga[t, :, 48:64] += edge_rows(1, 0, t)
        pre[t, :, 16:80] = ga[t] * pre[t, :, 16:80]
    edge_send(3, lambda side, t: pre[t, :, 16 + 48 * side : 32 + 48 * side])

    parts = (own_cells(0), own_cells(2))
    edge_wait(2)
    for t in range(8):
        for side in range(2):
            qh[side, t, :, :, 0:64] = edge_rows(2, 1 - side, t)
    for side in range(2):
        stack = jnp.concatenate(
            [stacked(lambda u: qh[side, u, :, :, 0:64], t).reshape(32, 192) for t in range(8)], axis=0
        ).astype(BF)
        hal3t = dot(eye_in[...], stack, NT).astype(BF)
        keep(2 * side, parts[side] + dot(hal3t, gh[side].reshape(256, 768), NN))
    for d in (2, 1, 3):
        x_copy(d, 1).start()
    zf[:, 56:64] = jnp.zeros((8, 8, 256), F32)
    zs[...] = zf[...].astype(BF)
    for d in (4, 3, 5, 2, 6, 1, 7):
        zz_copy(d).start()

    edge_wait(3)
    for t in range(8):
        pre[t, :, 0:16] = edge_rows(3, 1, t)
        pre[t, :, 80:96] = edge_rows(3, 0, t)

    col96 = lax.broadcasted_iota(jnp.int32, (192, 64), 0) % 16

    def shifted(t, _):
        part = pre[t].reshape(192, 64)
        after = jnp.where(col96 == 15, 0.0, pltpu.roll(part, 191, 0))
        before = jnp.where(col96 == 0, 0.0, pltpu.roll(part, 1, 0))
        gp3[t] = jnp.concatenate([after, part, before], axis=-1).reshape(2, 96, 192).astype(BF)
        return 0

    lax.fori_loop(0, 8, shifted, 0)
    gi[...] = jnp.zeros_like(gi)
    for a in range(3):
        n = 6 + a
        for b in range(3):
            k = 9 * a + 3 * b
            rows = gp3[2 - a : 8, :, 16 * (2 - b) : 16 * (2 - b) + 64, :].reshape(n * 128, 192)
            part = dot(rows, w[k : k + 3].reshape(192, 512), NN)
            gi[0:n] += part.reshape(n, 2, 64, 512)

    halves = (ylo, 1 - ylo)

    def pair_copy(half):
        return remote(pb.at[half], rp.at[half], pr_s.at[half], pr_r.at[half], dev(x, y, z, 1 - c))

    for half in halves:
        for f in range(2):
            pb[half, f] = gi[4 * half + 2 * (1 - c) + f].astype(BF)
        pair_copy(half).start()

    sbf[:, 40:48] = jnp.zeros((8, 8, 256), F32)

    def rows_of(i):
        return slice(16 * i, 16 + 32 * i)

    def z_copy(d, i):
        to = (z + d) % NZ
        part = rows_of(i)
        return remote(sb.at[to, part], rb.at[d - 1, part], b_s.at[d - 1, i], b_r.at[d - 1, i], dev(x, y, to, c))

    def x_sum(i):
        for d in range(1, 4):
            x_copy(d, i).wait_recv()
        for j in range(first_place[i], first_place[i] + size[i]):
            total = gws[5 * x + j].astype(F32)
            for d in range(3):
                total = total + ra[d, j].astype(F32)
            sbf[:, 8 * j : 8 * j + 8] = total.reshape(8, 8, 256)
        part = rows_of(i)
        sb[:, part] = sbf[:, part].astype(BF)
        for d in (4, 3, 5, 2, 6, 1, 7):
            z_copy(d, i).start()

    def z_sum(i):
        part = rows_of(i)
        for d in range(1, NZ):
            z_copy(d, i).wait_recv()
        total = sb[z, part].astype(F32)
        for d in range(NZ - 1):
            total = total + rb[d, part].astype(F32)
        fc[part] = (total * scale).astype(BF)

    x_sum(0)
    def y_copy(d):
        to = (y + d) % 4
        return remote(ps.at[to % 2, :, to // 2], rr.at[d - 1], rs_s.at[d - 1], rs_r.at[d - 1], dev(x, to, z, c))

    for half, steps in zip(halves, ((2,), (1, 3))):
        pair_copy(half).wait_recv()
        for f in range(2):
            ps[half, f] = (gi[4 * half + 2 * c + f] + rp[half, f].astype(F32)).astype(BF)
        for d in steps:
            y_copy(d).start()

    x_sum(1)
    for d in range(1, NZ):
        zz_copy(d).wait_recv()
    total = zs[z].astype(F32)
    for d in range(NZ - 1):
        total = total + rz[d].astype(F32)
    fz[...] = (total * scale).astype(BF)

    def mine(to_x):
        return jnp.logical_and(x == to_x, y == y_out)

    def out_z(to_x):
        return remote(fz, rcz.at[x], f_s.at[to_x], f_r.at[x], dev(to_x, y_out, z, c))

    for to_x in range(4):
        @pl.when(mine(to_x))
        def _():
            pltpu.make_async_copy(fz, rcz.at[x], f_r.at[x]).start()

        @pl.when(jnp.logical_not(mine(to_x)))
        def _():
            out_z(to_x).start()

    z_sum(0)
    z_sum(1)

    def out_copy(to_x):
        return remote(fc, rc.at[x], c_s.at[to_x], c_r.at[x], dev(to_x, y_out, z, c))

    for to_x in range(4):
        @pl.when(mine(to_x))
        def _():
            pltpu.make_async_copy(fc, rc.at[x], c_r.at[x]).start()

        @pl.when(jnp.logical_not(mine(to_x)))
        def _():
            out_copy(to_x).start()

    for d in range(1, 4):
        y_copy(d).wait_recv()
    total = ps[ylo, :, yhi].astype(F32)
    for d in range(3):
        total = total + rr[d].astype(F32)
    gi_out[...] = total.astype(BF)

    total = None
    for part in range(4):
        pltpu.make_async_copy(fz, rcz.at[part], f_r.at[part]).wait()
        v = rcz[part].astype(F32)
        total = v if total is None else total + v
    for m, (b, e, a) in enumerate(over_z):
        gw_out[9 * a + 3 * b + e] = total[8 * m : 8 * m + 8]
    for part in range(4):
        pltpu.make_async_copy(fc, rc.at[part], c_r.at[part]).wait()
        v = rc[part].astype(F32)
        for j in range(5):
            b, e, a = over_x[5 * part + j]
            gw_out[9 * a + 3 * b + e] = v[8 * j : 8 * j + 8]

    def sent(copy):
        copy.wait_send()

    for n in range(2):
        for i in range(10):
            gather(n, i).wait_send()
    for part in range(3):
        for slot in range(2):
            z_sends(part, slot, sent)
    for slot in range(2):
        @pl.when(pos != slot)
        def _():
            for i in range(6):
                along_x(slot, i).wait_send()

    for n in range(4):
        for side in range(2):
            edge_copy(n, side).wait_send()
    for half in halves:
        pair_copy(half).wait_send()
    for d in range(1, 4):
        for i in range(2):
            x_copy(d, i).wait_send()
        y_copy(d).wait_send()
    for d in range(1, NZ):
        zz_copy(d).wait_send()
        for i in range(2):
            z_copy(d, i).wait_send()
    for to_x in range(4):
        @pl.when(jnp.logical_not(mine(to_x)))
        def _():
            out_copy(to_x).wait_send()
            out_z(to_x).wait_send()


def on_device(latent, out_grad, w_first, w_second):
    wt = jnp.swapaxes(w_first, 1, 2)
    scale = 1.0 / math.sqrt(131072.0)
    hbm = pl.BlockSpec(memory_space=pl.ANY)
    vmem = pl.BlockSpec(memory_space=pltpu.VMEM)
    dma = pltpu.SemaphoreType.DMA
    grad_input, grad_w2 = pl.pallas_call(
        functools.partial(body, scale),
        out_shape=(
            jax.ShapeDtypeStruct((2, 64, 512), BF),
            jax.ShapeDtypeStruct((27, 8, 256), F32),
        ),
        in_specs=[hbm, hbm, hbm, hbm, vmem, vmem],
        out_specs=(vmem, vmem),
        scratch_shapes=[
            pltpu.VMEM((8, 2, 64, 512), BF),
            pltpu.VMEM((8, 2, 256, 256), BF),
            pltpu.VMEM((27, 2, 32, 512), BF),
            pltpu.VMEM((192, 2304), BF),
            pltpu.VMEM((8, 2, 64, 2304), BF),
            pltpu.VMEM((2, 8, 2, 16, 768), BF),
            pltpu.VMEM((8, 2, 64, 192), F32),
            pltpu.VMEM((2, 8, 2, 16, 192), F32),
            pltpu.VMEM((8, 2, 64, 192), F32),
            pltpu.VMEM((2, 8, 2, 16, 192), F32),
            pltpu.VMEM((8, 2, 96, 64), F32),
            pltpu.VMEM((8, 2, 64, 64), F32),
            pltpu.VMEM((4, 2, 4, 2, 16, 128), BF),
            pltpu.VMEM((4, 2, 4, 2, 16, 128), BF),
            pltpu.VMEM((8, 2, 64, 64), F32),
            pltpu.VMEM((8, 2, 96, 192), BF),
            pltpu.VMEM((8, 2, 64, 192), BF),
            pltpu.VMEM((192, 1024), BF),
            pltpu.VMEM((8, 2, 64, 512), F32),
            pltpu.VMEM((2, 2, 2, 64, 512), BF),
            pltpu.VMEM((2, 2, 2, 64, 512), BF),
            pltpu.VMEM((2, 2, 2, 64, 512), BF),
            pltpu.VMEM((3, 2, 64, 512), BF),
            pltpu.VMEM((20, 64, 256), BF),
            pltpu.VMEM((3, 5, 64, 256), BF),
            pltpu.VMEM((8, 48, 256), F32),
            pltpu.VMEM((8, 48, 256), BF),
            pltpu.VMEM((7, 48, 256), BF),
            pltpu.VMEM((48, 256), BF),
            pltpu.VMEM((4, 48, 256), BF),
            pltpu.VMEM((8, 64, 256), F32),
            pltpu.VMEM((8, 64, 256), BF),
            pltpu.VMEM((7, 64, 256), BF),
            pltpu.VMEM((64, 256), BF),
            pltpu.VMEM((4, 64, 256), BF),
            dma((3,)), dma((3, 9)),
            dma((2, 10)), dma((2, 10)),
            dma((3, 2, 4)), dma((3, 2)),
            dma((2, 6)), dma((2, 6)),
            dma((4, 2)), dma((4, 2)),
            dma((2,)), dma((2,)),
            dma((3,)), dma((3,)),
            dma((3, 2)), dma((3, 2)),
            dma((7, 2)), dma((7, 2)),
            dma((4,)), dma((4,)),
            dma((7,)), dma((7,)),
            dma((4,)), dma((4,)),
        ],
        compiler_params=pltpu.CompilerParams(
            collective_id=0, has_side_effects=True, vmem_limit_bytes=56 * 1024 * 1024
        ),
    )(
        latent.reshape(2, 64, 512),
        out_grad.reshape(2, 256, 256),
        wt,
        w_second,
        jnp.asarray(cell_sums(), BF),
        jnp.asarray(np.eye(192, dtype=np.float32), BF),
    )
    return grad_input.reshape(1, 2, 4, 16, 512), jnp.swapaxes(grad_w2, 0, 1)


def solution(mesh):
    placed = (
        P("dp", "tm", "height", None, None),
        P("dp", "tm", "height", None, None),
        P(None, None, "height"),
        P(),
    )
    return jax.shard_map(
        on_device,
        mesh=mesh,
        in_specs=placed,
        out_specs=(P("dp", "tm", "height", None, None), P(("tm", "height"), None, None)),
        check_vma=False,
    )
```
